128 devices in a mesh: chan: 64 (over z, y, x), dom: 2 (over core).
Axes of the slice: x: 4, y: 4, z: 4, core: 2. Of those that a mesh axis runs over, the one named last changes fastest.
Arguments:
- amplitudes: bfloat16 [128, 2048, 512], P('chan', None, 'dom'), may hold values from -6 to 6
- recouple: bfloat16 [128, 2048, 2048], P('chan'), may hold values from -0.125 to 0.125
- ladder_int: bfloat16 [128, 2048, 2048], P('chan'), may hold values from -0.125 to 0.125
- cycle_coupling: bfloat16 [128, 512, 512], P('chan', 'dom'), may hold values from -0.375 to 0.375
- drive: bfloat16 [128, 2048, 512], P('chan', None, 'dom'), may hold values from -6 to 6
- eps_part: float32 [128, 2048], P('chan'), may hold values from 0.5 to 2.5
- eps_hole: float32 [128, 512], P('chan', 'dom'), may hold values from -2.5 to -0.5
Outputs:
- new_amplitudes: bfloat16 [128, 2048, 512], P('chan', None, 'dom')
The draws below stay inside these ranges and needn't reach their ends.
All inputs are finite; a program needn't handle non-finite values.
Results may differ from the reference program's by a relative error of at most 0.0052.
Values may be sent and summed in bfloat16 or wider, within the bound.
No kernel may reach another device: no remote copies, remote signals or barrier semaphores. Data moves between devices by JAX's collectives and lax.ppermute only.
A program may use at most 128 MiB of HBM per device.

```python
import jax
import jax.numpy as jnp

P_SIZE = 2048
H = 512
CH_DEV = 2
CHANNELS = 128
N_CHAN = 64


def strengthened(array, key, source, target, blocks, factor):
    owner, partner = [(jnp.arange(array.shape[axis_at]) // (array.shape[axis_at] // blocks)).reshape([-1 if axis == axis_at else 1 for axis in range(array.ndim)]) for axis_at in (source, target)]
    chosen = jax.random.permutation(key, blocks)[partner]
    strong = (owner == chosen) | (owner == (partner + blocks // 2) % blocks)
    return jnp.where(strong, factor * array, array)


def block_levels(stream_key, dims, split, least, top_value):
    def one(position, blocks):
        steps = jax.random.uniform(jax.random.fold_in(jax.random.fold_in(stream_key, 6), position), (blocks,), jnp.float32, least / len(split), top_value / len(split))
        return jnp.repeat(jnp.exp(steps), dims[position] // blocks).reshape((-1,) + (1,) * (len(dims) - position - 1))

    loudness = one(*split[0])
    for cut in split[1:]:
        loudness = loudness * one(*cut)
    return loudness


def noise(own_key, extent, scale, reach, shards=(), dtype=jnp.bfloat16):
    loudness = block_levels(own_key, extent, shards, -0.22, 0.18) if shards else 1.0
    array = jax.random.normal(own_key, extent, jnp.float32) * scale * loudness
    return jnp.minimum(jnp.maximum(array, -reach), reach).astype(dtype)


def noise_with(own_key, dims, deviation, most, shards, heavy, held_as=jnp.bfloat16):
    array = deviation * jax.random.normal(own_key, dims, jnp.float32)
    if shards:
        array = array * block_levels(own_key, dims, shards, -0.22, 0.18)
    return jnp.clip(strengthened(array, jax.random.fold_in(own_key, 3), *heavy), -most, most).astype(held_as)


def setup_inputs(seed: int = 0) -> dict:
    streams_of = jax.random.split(jax.random.key(seed), 8)
    return {
        "amplitudes": noise(streams_of[0], (CHANNELS, P_SIZE, H), 1.0, 6.0, ((0, 64), (2, 2))),
        "recouple": noise(streams_of[1], (CHANNELS, P_SIZE, P_SIZE), P_SIZE ** -0.5, 0.125, ((0, 64),)),
        "ladder_int": noise(streams_of[2], (CHANNELS, P_SIZE, P_SIZE), P_SIZE ** -0.5, 0.125, ((0, 64),)),
        "cycle_coupling": noise_with(streams_of[3], (CHANNELS, H, H), H ** -0.5, 0.375, ((0, 64), (1, 2)), (1, 2, 2, 2.0)),
        "drive": noise(streams_of[4], (CHANNELS, P_SIZE, H), 1.0, 6.0, ((0, 64), (2, 2))),
        "eps_part": jnp.clip(0.5 + 2.0 * jax.random.uniform(streams_of[5], (CHANNELS, P_SIZE), jnp.float32) ** block_levels(streams_of[5], (CHANNELS, P_SIZE), ((0, 64),), -0.2, 0.2), 0.5, 2.5),
        "eps_hole": jnp.clip(-2.5 + 2.0 * jax.random.uniform(streams_of[6], (CHANNELS, H), jnp.float32) ** block_levels(streams_of[6], (CHANNELS, H), ((0, 64), (1, 2)), -0.2, 0.2), -2.5, -0.5),
    }


def regroup(blocks):
    seg_rows = P_SIZE // N_CHAN
    shaped = blocks.reshape(N_CHAN, CH_DEV, N_CHAN, seg_rows, H)
    return shaped.transpose(2, 1, 0, 3, 4).reshape(CHANNELS, P_SIZE, H)


def reference(amplitudes, recouple, ladder_int, cycle_coupling, drive, eps_part, eps_hole):
    amp_wide = amplitudes.astype(jnp.float32)
    coeff_wide = recouple.astype(jnp.float32)
    recoupled = jnp.einsum('cpq,cqh->cph', coeff_wide, amp_wide).astype(jnp.bfloat16)
    ph_blocks = regroup(recoupled)
    cycle_term = jnp.einsum('cph,chk->cpk', ph_blocks.astype(jnp.float32), cycle_coupling.astype(jnp.float32)).astype(jnp.bfloat16)
    returned = regroup(cycle_term)
    ladder = jnp.einsum('cpq,cqh->cph', ladder_int.astype(jnp.float32), amp_wide)
    folded = jnp.einsum('cqp,cqh->cph', coeff_wide, returned.astype(jnp.float32))
    summed = ladder + folded + drive.astype(jnp.float32)
    denominator = eps_part[:, :, None] - eps_hole[:, None, :]
    return (summed / denominator).astype(jnp.bfloat16)
```

```python
import itertools

import jax
import jax.numpy as jnp
from jax import lax
from jax.experimental import pallas as pl
from jax.experimental.pallas import tpu as pltpu
from jax.sharding import PartitionSpec as P

RING = ((0, 0), (0, 1), (1, 1), (1, 0))
PLACE = {bits: at for at, bits in enumerate(RING)}
BF, F32 = jnp.bfloat16, jnp.float32
WIDE = 48 * 1024 * 1024


def chip(bits):
    return (PLACE[bits[0]] * 4 + PLACE[bits[1]]) * 4 + PLACE[bits[2]]


def bits_of(core, moved, kept):
    return [(m, k) if core == 0 else (k, m) for m, k in zip(moved, kept)]


THREE = list(itertools.product((0, 1), repeat=3))
GROUPS = [
    [chip(bits_of(core, moved, kept)) * 2 + core for moved in THREE]
    for core in range(2)
    for kept in THREE
]


def flips(axis):
    pairs = []
    for core, moved, kept in itertools.product(range(2), THREE, THREE):
        other = [k ^ (a == axis) for a, k in enumerate(kept)]
        pairs.append(
            (
                chip(bits_of(core, moved, kept)) * 2 + core,
                chip(bits_of(core, moved, other)) * 2 + core,
            )
        )
    return pairs


FLIPS = [flips(axis) for axis in range(3)]
BOTH = ("chan", "dom")


def swap(array):
    return lax.ppermute(array, "dom", [(0, 1), (1, 0)])


def over(array, axis):
    return lax.ppermute(array, BOTH, FLIPS[axis])


def segment(core, moved, kept):
    at = 0
    for shift in (2, 1, 0):
        m, k = (moved >> shift) & 1, (kept >> shift) & 1
        at = at * 4 + 2 * jnp.where(core == 0, m, k) + (m ^ k)
    return at


def dot(a, b):
    return jnp.dot(a, b, preferred_element_type=F32)


def params():
    return pltpu.CompilerParams(vmem_limit_bytes=WIDE)


def cost(flops, moved):
    return pl.CostEstimate(flops=flops, bytes_accessed=moved, transcendentals=0)


def row_specs(rows, width):
    return [
        pl.BlockSpec((1, rows, width), lambda m, sc, k=k: (sc[0], segment(sc[0], m, k), 0))
        for k in range(8)
    ]


def recoupled_kernel(sc, *refs):
    own, oth, out = refs[8:]
    rows = jnp.concatenate([ref[0] for ref in refs[:8]], axis=0)
    half = own.shape[2]
    out[0, :, :half] = dot(rows, own[0]).astype(BF)
    out[0, :, half:] = dot(rows, oth[...]).astype(BF)


def recoupled_call(sc, recouple, amplitudes, other):
    _, n, _ = recouple.shape
    half = amplitudes.shape[2]
    return pl.pallas_call(
        recoupled_kernel,
        grid_spec=pltpu.PrefetchScalarGridSpec(
            num_scalar_prefetch=1,
            grid=(8,),
            in_specs=row_specs(n // 64, n)
            + [
                pl.BlockSpec((1, n, half), lambda m, sc: (sc[0], 0, 0)),
                pl.BlockSpec((n, half), lambda m, sc: (0, 0)),
            ],
            out_specs=pl.BlockSpec((1, n // 8, 2 * half), lambda m, sc: (m, 0, 0)),
        ),
        out_shape=jax.ShapeDtypeStruct((8, n // 8, 2 * half), BF),
        compiler_params=params(),
        cost_estimate=cost(4 * n * n * half, 2 * n * n + 8 * n * half),
        name="recoupled",
    )(sc, *([recouple] * 8), amplitudes, other)


def turn_kernel(sc, *refs):
    rows = jnp.concatenate([ref[0] for ref in refs[:8]], axis=0)
    refs[8][...] = rows.T


def turn_call(sc, recouple):
    _, n, _ = recouple.shape
    return pl.pallas_call(
        turn_kernel,
        grid_spec=pltpu.PrefetchScalarGridSpec(
            num_scalar_prefetch=1,
            grid=(8,),
            in_specs=row_specs(n // 64, n),
            out_specs=pl.BlockSpec((n, n // 8), lambda m, sc: (0, m)),
        ),
        out_shape=jax.ShapeDtypeStruct((n, n), BF),
        compiler_params=params(),
        cost_estimate=cost(0, 4 * n * n),
        name="turned",
    )(sc, *([recouple] * 8))


def cycle_kernel(sc, x, c, out):
    rows, half = x.shape[0] * x.shape[2], c.shape[2] // 2
    lines = x[...].reshape(rows, x.shape[3])
    for side in range(2):
        at = pl.multiple_of((sc[0] ^ side) * half, half)
        got = dot(lines, c[0, :, pl.ds(at, half)]).astype(BF)
        out[:, :, :, side * half : (side + 1) * half] = got.reshape(x.shape[:3] + (half,))


def cycle_call(sc, blocks, couplings):
    _, _, rows, h = blocks.shape
    spec = pl.BlockSpec((8, 1, rows, h), lambda r, sc: (0, r ^ sc[1], 0, 0))
    return pl.pallas_call(
        cycle_kernel,
        grid_spec=pltpu.PrefetchScalarGridSpec(
            num_scalar_prefetch=1,
            grid=(8,),
            in_specs=[spec, pl.BlockSpec((1, h, h), lambda r, sc: (r, 0, 0))],
            out_specs=spec,
        ),
        out_shape=jax.ShapeDtypeStruct(blocks.shape, BF),
        compiler_params=params(),
        cost_estimate=cost(2 * 64 * rows * h * h, 256 * rows * h + 16 * h * h),
        name="cycle",
    )(sc, blocks, couplings)


def ladder_kernel(sc, l, own, oth, drive, drive_oth, out):
    half = own.shape[2]
    out[:, :half] = dot(l[0], own[0]) + drive[0].astype(F32)
    out[:, half:] = dot(l[0], oth[...]) + drive_oth[...].astype(F32)


def ladder_call(sc, ladder_int, amplitudes, other, drive, drive_other):
    _, n, _ = ladder_int.shape
    half = amplitudes.shape[2]
    tile = n // 8
    return pl.pallas_call(
        ladder_kernel,
        grid_spec=pltpu.PrefetchScalarGridSpec(
            num_scalar_prefetch=1,
            grid=(8,),
            in_specs=[
                pl.BlockSpec((1, tile, n), lambda i, sc: (sc[0], i, 0)),
                pl.BlockSpec((1, n, half), lambda i, sc: (sc[0], 0, 0)),
                pl.BlockSpec((n, half), lambda i, sc: (0, 0)),
                pl.BlockSpec((1, tile, half), lambda i, sc: (sc[0], i, 0)),
                pl.BlockSpec((tile, half), lambda i, sc: (i, 0)),
            ],
            out_specs=pl.BlockSpec((tile, 2 * half), lambda i, sc: (i, 0)),
        ),
        out_shape=jax.ShapeDtypeStruct((n, 2 * half), F32),
        compiler_params=params(),
        cost_estimate=cost(4 * n * n * half, 2 * n * n + 16 * n * half),
        name="ladder",
    )(sc, ladder_int, amplitudes, other, drive, drive_other)


def final_kernel(sc, turned, x, ladder, part, hole, out, out_oth):
    half = out.shape[2]
    for side, to in ((1, out_oth), (0, out)):
        at = slice(side * half, (side + 1) * half)
        total = dot(turned[...], x[:, at]) + ladder[:, at]
        got = (total / (part[...] - hole[:, at])).astype(BF)
        to[...] = got.reshape(to.shape)


def final_call(sc, turned, returned, ladder, part, hole):
    n, h = returned.shape
    tile, half = n // 8, h // 2
    return pl.pallas_call(
        final_kernel,
        grid_spec=pltpu.PrefetchScalarGridSpec(
            num_scalar_prefetch=1,
            grid=(8,),
            in_specs=[
                pl.BlockSpec((tile, n), lambda i, sc: (i, 0)),
                pl.BlockSpec((n, h), lambda i, sc: (0, 0)),
                pl.BlockSpec((tile, h), lambda i, sc: (i, 0)),
                pl.BlockSpec((tile, 1), lambda i, sc: (i, 0)),
                pl.BlockSpec((1, h), lambda i, sc: (0, 0)),
            ],
            out_specs=[
                pl.BlockSpec((1, tile, half), lambda i, sc: (sc[0], i, 0)),
                pl.BlockSpec((tile, half), lambda i, sc: (i, 0)),
            ],
        ),
        out_shape=[
            jax.ShapeDtypeStruct((2, n, half), BF),
            jax.ShapeDtypeStruct((n, half), BF),
        ],
        compiler_params=params(),
        cost_estimate=cost(2 * n * n * h, 2 * n * n + 8 * n * h),
        name="final",
    )(sc, turned, returned, ladder, part, hole)


def local(amplitudes, recouple, ladder_int, cycle_coupling, drive, eps_part, eps_hole):
    _, n, half = amplitudes.shape
    h, seg = 2 * half, n // 64
    core, here = lax.axis_index("dom"), lax.axis_index("chan")
    kept = 0
    for weight in (16, 4, 1):
        place = (here // weight) % 4
        high, low = place // 2, ((place + 1) // 2) % 2
        kept = 2 * kept + jnp.where(core == 0, low, high)
    sc = jnp.stack([core, kept]).astype(jnp.int32)

    def mine(array):
        return lax.dynamic_index_in_dim(array, core, 0, keepdims=False)

    def others(array):
        return swap(lax.dynamic_index_in_dim(array, 1 - core, 0, keepdims=False))

    amp_other = others(amplitudes)
    c0 = jnp.concatenate([mine(cycle_coupling), others(cycle_coupling)], axis=0)
    hole = jnp.concatenate([mine(eps_hole), others(eps_hole)])[None, :]
    part = mine(eps_part)[:, None]
    drive_other = others(drive)

    recoupled = recoupled_call(sc, recouple, amplitudes, amp_other)

    c4, c2, c1 = over(c0, 0), over(c0, 1), over(c0, 2)
    c6, c3, c5 = over(c4, 1), over(c2, 2), over(c1, 0)
    c7 = over(c6, 2)
    couplings = jnp.stack([c0, c1, c2, c3, c4, c5, c6, c7])

    def exchange(array):
        return lax.all_to_all(array, BOTH, 0, 0, axis_index_groups=GROUPS, tiled=True)

    blocks = exchange(recoupled).reshape(8, 8, seg, h)
    turned = turn_call(sc, recouple)
    ladder = ladder_call(sc, ladder_int, amplitudes, amp_other, drive, drive_other)
    cycle_term = cycle_call(sc, blocks, couplings)
    returned = exchange(cycle_term.reshape(8, 8 * seg, h)).reshape(n, h)
    out, out_other = final_call(sc, turned, returned, ladder, part, hole)
    return lax.dynamic_update_slice(out, swap(out_other)[None], (1 - core, 0, 0))


def solution(mesh):
    placed = (
        P("chan", None, "dom"),
        P("chan", None, None),
        P("chan", None, None),
        P("chan", "dom", None),
        P("chan", None, "dom"),
        P("chan", None),
        P("chan", "dom"),
    )
    return jax.shard_map(
        local, mesh=mesh, in_specs=placed, out_specs=P("chan", None, "dom"), check_vma=False
    )
```

```python
import itertools

import jax
import jax.numpy as jnp
from jax import lax
from jax.experimental import pallas as pl
from jax.experimental.pallas import tpu as pltpu
from jax.sharding import PartitionSpec as P

RING = ((0, 0), (0, 1), (1, 1), (1, 0))
PLACE = {bits: at for at, bits in enumerate(RING)}
BF, F32 = jnp.bfloat16, jnp.float32
VMEM = pltpu.VMEM


def chip(bits):
    return (PLACE[bits[0]] * 4 + PLACE[bits[1]]) * 4 + PLACE[bits[2]]


def bits_of(core, moved, kept):
    return [(m, k) if core == 0 else (k, m) for m, k in zip(moved, kept)]


THREE = list(itertools.product((0, 1), repeat=3))
GROUPS = [
    [chip(bits_of(core, moved, kept)) * 2 + core for moved in THREE]
    for core in range(2)
    for kept in THREE
]


def flips(axis):
    pairs = []
    for core, moved, kept in itertools.product(range(2), THREE, THREE):
        other = [k ^ (a == axis) for a, k in enumerate(kept)]
        pairs.append(
            (
                chip(bits_of(core, moved, kept)) * 2 + core,
                chip(bits_of(core, moved, other)) * 2 + core,
            )
        )
    return pairs


FLIPS = [flips(axis) for axis in range(3)]
BOTH = ("chan", "dom")


def swap(array):
    return lax.ppermute(array, "dom", [(0, 1), (1, 0)])


def over(array, axis):
    return lax.ppermute(array, BOTH, FLIPS[axis])


def slot(core, chip_at):
    places = [(chip_at >> shift) & 3 for shift in (4, 2, 0)]
    at = []
    for c in range(2):
        moved = [RING[p][c] for p in places]
        kept = [RING[p][1 - c] for p in places]
        at.append(sum(b << (5 - i) for i, b in enumerate(moved + kept)))
    return at[0] + core * (at[1] - at[0])


def dot(a, b):
    return jnp.dot(a, b, preferred_element_type=F32)


def params(mib):
    return pltpu.CompilerParams(vmem_limit_bytes=mib * 1024 * 1024)


def cost(flops, moved):
    return pl.CostEstimate(flops=flops, bytes_accessed=moved, transcendentals=0)


def held(array):
    return pltpu.with_memory_space_constraint(array, VMEM)


def far(array):
    return pltpu.with_memory_space_constraint(array, pltpu.HBM)


WHOLE = pl.BlockSpec(memory_space=VMEM)
AWAY = pl.BlockSpec(memory_space=pltpu.HBM)
TILES = 4


def scatter(core, got, tile, send, columns):
    seg = send.shape[1]
    each = got.shape[0] // seg
    for j in range(each):
        send[slot(core, tile * each + j), :, columns] = got[j * seg : (j + 1) * seg]


def own_kernel(sc, recouple, amplitudes, rows, send, amp, sems):
    core, n, half = sc[0], rows.shape[0], amp.shape[1]
    tile = n // TILES
    copies = [pltpu.make_async_copy(amplitudes.at[core], amp, sems.at[TILES])]
    for i in range(TILES):
        at = pl.ds(i * tile, tile)
        copies.append(pltpu.make_async_copy(recouple.at[core, at], rows.at[at], sems.at[i]))
    for copy in copies:
        copy.start()
    copies[0].wait()
    for i in range(TILES):
        copies[1 + i].wait()
        got = dot(rows[i * tile : (i + 1) * tile], amp[...]).astype(BF)
        scatter(core, got, i, send, slice(0, half))


def own_call(sc, recouple, amplitudes):
    _, n, half = amplitudes.shape
    return pl.pallas_call(
        own_kernel,
        grid_spec=pltpu.PrefetchScalarGridSpec(
            num_scalar_prefetch=1,
            grid=(1,),
            in_specs=[AWAY, AWAY],
            out_specs=[WHOLE, WHOLE],
            scratch_shapes=[VMEM((n, half), BF), pltpu.SemaphoreType.DMA((TILES + 1,))],
        ),
        out_shape=[VMEM((n, n), BF), VMEM((64, n // 64, 2 * half), BF)],
        compiler_params=params(16),
        cost_estimate=cost(2 * n * n * half, 2 * n * n),
        name="recoupled_own",
    )(sc, far(recouple), far(amplitudes))


def other_kernel(sc, rows, amp, given, send):
    tile, half = rows.shape[0] // TILES, amp.shape[2]
    for i in range(TILES):
        got = dot(rows[i * tile : (i + 1) * tile], amp[0]).astype(BF)
        scatter(sc[0], got, i, send, slice(half, 2 * half))


def other_call(sc, rows, amp_other, send):
    _, n, half = amp_other.shape
    return pl.pallas_call(
        other_kernel,
        grid_spec=pltpu.PrefetchScalarGridSpec(
            num_scalar_prefetch=1,
            grid=(1,),
            in_specs=[WHOLE, pl.BlockSpec((1, n, half), lambda i, sc: (sc[0], 0, 0)), WHOLE],
            out_specs=WHOLE,
        ),
        out_shape=VMEM(send.shape, BF),
        input_output_aliases={3: 0},
        compiler_params=params(16),
        cost_estimate=cost(2 * n * n * half, 4 * n * half),
        name="recoupled_other",
    )(sc, held(rows), amp_other, held(send))


def coupling_kernel(sc, own, oth, out):
    half, h = own.shape[1:]
    for core in range(2):

        @pl.when(sc[0] == core)
        def _():
            for part, ref in enumerate((own, oth)):
                for side in range(2):
                    at = (core ^ side) * half
                    out[part * half : (part + 1) * half, side * half : (side + 1) * half] = ref[
                        0, :, at : at + half
                    ]


def coupling_call(sc, own, oth):
    _, half, h = own.shape
    spec = pl.BlockSpec((1, half, h), lambda i, sc: (sc[0], 0, 0))
    return pl.pallas_call(
        coupling_kernel,
        grid_spec=pltpu.PrefetchScalarGridSpec(
            num_scalar_prefetch=1, grid=(1,), in_specs=[spec, spec], out_specs=WHOLE
        ),
        out_shape=VMEM((h, h), BF),
        compiler_params=params(8),
        cost_estimate=cost(0, 4 * h * h),
        name="coupling",
    )(sc, own, oth)


def cycle_kernel(sc, x, *refs):
    out = refs[8]
    lines = (x.shape[0] * x.shape[2], x.shape[3])
    for r in range(8):
        at = r ^ sc[1]
        got = dot(x[:, at].reshape(lines), refs[r][...]).astype(BF)
        out[:, at] = got.reshape(x.shape[0], x.shape[2], x.shape[3])


def cycle_call(sc, blocks, couplings):
    _, _, rows, h = blocks.shape
    return pl.pallas_call(
        cycle_kernel,
        grid_spec=pltpu.PrefetchScalarGridSpec(
            num_scalar_prefetch=1, grid=(1,), in_specs=[WHOLE] * 9, out_specs=WHOLE
        ),
        out_shape=VMEM(blocks.shape, BF),
        compiler_params=params(8),
        cost_estimate=cost(2 * 64 * rows * h * h, 256 * rows * h + 16 * h * h),
        name="cycle",
    )(sc, held(blocks), *[held(c) for c in couplings])


def ladder_kernel(sc, l, own, oth, drive, drive_oth, part, out, out_part):
    half, tile = own.shape[2], l.shape[1]
    at = pl.ds(pl.multiple_of(pl.program_id(0) * tile, tile), tile)
    out[at, :half] = dot(l[0], own[0]) + drive[0].astype(F32)
    out[at, half:] = dot(l[0], oth[0]) + drive_oth[0].astype(F32)
    out_part[at, :] = jnp.broadcast_to(part[pl.ds(sc[0], 1), :], (128, tile)).T


def ladder_call(sc, ladder_int, amplitudes, amp_other, drive, drive_other, eps_part):
    _, n, half = amplitudes.shape
    tile = n // TILES
    whole = pl.BlockSpec((1, n, half), lambda i, sc: (sc[0], 0, 0))
    piece = pl.BlockSpec((1, tile, half), lambda i, sc: (sc[0], i, 0))
    return pl.pallas_call(
        ladder_kernel,
        grid_spec=pltpu.PrefetchScalarGridSpec(
            num_scalar_prefetch=1,
            grid=(TILES,),
            in_specs=[
                pl.BlockSpec((1, tile, n), lambda i, sc: (sc[0], i, 0)),
                whole,
                whole,
                piece,
                piece,
                pl.BlockSpec((2, tile), lambda i, sc: (0, i)),
            ],
            out_specs=[WHOLE, WHOLE],
        ),
        out_shape=[VMEM((n, 2 * half), F32), VMEM((n, 128), F32)],
        compiler_params=params(20),
        cost_estimate=cost(4 * n * n * half, 2 * n * n + 16 * n * half),
        name="ladder",
    )(sc, far(ladder_int), amplitudes, amp_other, drive, drive_other, eps_part)


def final_kernel(sc, rows, x, ladder, part, hole, hole_oth, out, out_oth, lines):
    core, i = sc[0], pl.program_id(0)
    half, tile, seg = out.shape[2], out.shape[1], x.shape[1]

    @pl.when(i == 0)
    def _():
        for at in range(64):
            lines[at * seg : (at + 1) * seg, :] = x[slot(core, at)]

    at = pl.ds(pl.multiple_of(i * tile, tile), tile)
    low = part[at, :1]
    for side, to, eps in ((1, out_oth, hole_oth), (0, out, hole)):
        cols = slice(side * half, (side + 1) * half)
        total = lax.dot_general(
            rows[:, at], lines[:, cols], (((0,), (0,)), ((), ())), preferred_element_type=F32
        )
        total = total + ladder[at, cols]
        got = (total / (low - eps[pl.ds(core, 1), :])).astype(BF)
        to[...] = got.reshape(to.shape)


def final_call(sc, rows, returned, ladder, part, hole, hole_other):
    n, h = ladder.shape
    tile, half = n // TILES, h // 2
    return pl.pallas_call(
        final_kernel,
        grid_spec=pltpu.PrefetchScalarGridSpec(
            num_scalar_prefetch=1,
            grid=(TILES,),
            in_specs=[WHOLE] * 6,
            out_specs=[
                pl.BlockSpec((1, tile, half), lambda i, sc: (sc[0], i, 0)),
                pl.BlockSpec((tile, half), lambda i, sc: (i, 0)),
            ],
            scratch_shapes=[VMEM((n, h), BF)],
        ),
        out_shape=[
            jax.ShapeDtypeStruct((2, n, half), BF),
            jax.ShapeDtypeStruct((n, half), BF),
        ],
        compiler_params=params(16),
        cost_estimate=cost(2 * n * n * h, 6 * n * h),
        name="final",
    )(sc, held(rows), held(returned), held(ladder), held(part), held(hole), held(hole_other))


def local(amplitudes, recouple, ladder_int, cycle_coupling, drive, eps_part, eps_hole):
    _, n, half = amplitudes.shape
    core, here = lax.axis_index("dom"), lax.axis_index("chan")
    kept = 0
    for weight in (16, 4, 1):
        place = (here // weight) % 4
        high, low = place // 2, ((place + 1) // 2) % 2
        kept = 2 * kept + jnp.where(core == 0, low, high)
    sc = jnp.stack([core, kept]).astype(jnp.int32)

    amp_other = swap(amplitudes)
    rows, send = own_call(sc, recouple, amplitudes)
    c0 = coupling_call(sc, cycle_coupling, swap(cycle_coupling))
    send = other_call(sc, rows, amp_other, send)

    c4, c2, c1 = over(c0, 0), over(c0, 1), over(c0, 2)
    c6, c3, c5 = over(c4, 1), over(c2, 2), over(c1, 0)
    c7 = over(c6, 2)

    def exchange(array):
        return lax.all_to_all(array, BOTH, 0, 0, axis_index_groups=GROUPS, tiled=True)

    blocks = exchange(send)
    ladder, part = ladder_call(
        sc, ladder_int, amplitudes, amp_other, drive, swap(drive), eps_part
    )
    cycle_term = cycle_call(
        sc, blocks.reshape((8, 8) + blocks.shape[1:]), [c0, c1, c2, c3, c4, c5, c6, c7]
    )
    returned = exchange(cycle_term.reshape(blocks.shape))
    out, out_other = final_call(sc, rows, returned, ladder, part, eps_hole, swap(eps_hole))
    return lax.dynamic_update_slice(out, swap(out_other)[None], (1 - core, 0, 0))


def solution(mesh):
    placed = (
        P("chan", None, "dom"),
        P("chan", None, None),
        P("chan", None, None),
        P("chan", "dom", None),
        P("chan", None, "dom"),
        P("chan", None),
        P("chan", "dom"),
    )
    return jax.shard_map(
        local, mesh=mesh, in_specs=placed, out_specs=P("chan", None, "dom"), check_vma=False
    )
```

```python
import functools
import itertools

import jax
import jax.numpy as jnp
from jax import lax
from jax.experimental import pallas as pl
from jax.experimental.pallas import tpu as pltpu
from jax.sharding import PartitionSpec as P

RING = ((0, 0), (0, 1), (1, 1), (1, 0))
PLACE = {bits: at for at, bits in enumerate(RING)}
BF, F32 = jnp.bfloat16, jnp.float32
VMEM = pltpu.VMEM


def chip(bits):
    return (PLACE[bits[0]] * 4 + PLACE[bits[1]]) * 4 + PLACE[bits[2]]


def bits_of(core, moved, kept):
    return [(m, k) if core == 0 else (k, m) for m, k in zip(moved, kept)]


THREE = list(itertools.product((0, 1), repeat=3))
def flips(of_moved, of_kept):
    pairs = []
    for core, moved, kept in itertools.product(range(2), THREE, THREE):
        to = [m ^ f for m, f in zip(moved, THREE[of_moved])]
        at = [k ^ f for k, f in zip(kept, THREE[of_kept])]
        pairs.append(
            (
                chip(bits_of(core, moved, kept)) * 2 + core,
                chip(bits_of(core, to, at)) * 2 + core,
            )
        )
    return pairs


BOTH = ("chan", "dom")


def swap(array):
    return lax.ppermute(array, "dom", [(0, 1), (1, 0)])


def over(array, moved=0, kept=0):
    return lax.ppermute(array, BOTH, flips(moved, kept))


def segment(core, moved, kept):
    at = 0
    for shift in (2, 1, 0):
        m, k = (moved >> shift) & 1, (kept >> shift) & 1
        at = at * 4 + 2 * jnp.where(core == 0, m, k) + (m ^ k)
    return at


def dot(a, b):
    return jnp.dot(a, b, preferred_element_type=F32)


def dot_rows(a, b):
    return lax.dot_general(a, b, (((0,), (0,)), ((), ())), preferred_element_type=F32)


def params(mib):
    return pltpu.CompilerParams(vmem_limit_bytes=mib * 1024 * 1024)


def cost(flops, moved):
    return pl.CostEstimate(flops=flops, bytes_accessed=moved, transcendentals=0)


def held(array):
    return pltpu.with_memory_space_constraint(array, VMEM)


def far(array):
    return pltpu.with_memory_space_constraint(array, pltpu.HBM)


WHOLE = pl.BlockSpec(memory_space=VMEM)
AWAY = pl.BlockSpec(memory_space=pltpu.HBM)
WAIT = pl.BlockSpec(memory_space=pl.ANY)
TILES = 4
FIRST, THEN = (7, 1), (3, 5, 6, 2, 4)
BACK = (0, 7, 3, 5, 1), (6, 2, 4)
EARLY, LATE = (0, 7, 3, 5), (1, 6, 2, 4)


def tie_kernel(*refs):
    pass


def tie(arrays, *waits):
    count = len(arrays)
    return pl.pallas_call(
        tie_kernel,
        in_specs=[WAIT] * (count + len(waits)),
        out_specs=[WAIT] * count,
        out_shape=[jax.ShapeDtypeStruct(a.shape, a.dtype) for a in arrays],
        input_output_aliases={i: i for i in range(count)},
        compiler_params=params(1),
        cost_estimate=cost(0, 0),
        name="tie",
    )(*arrays, *waits)


def load_kernel(sc, recouple, amplitudes, drive, rows, amp, amp_send, drive_send, sems):
    core, seg = sc[0], rows.shape[0] // 64
    copies = [
        pltpu.make_async_copy(source, to, sems.at[64 + i])
        for i, (source, to) in enumerate(
            (
                (amplitudes.at[1 - core], amp_send),
                (drive.at[1 - core], drive_send),
                (amplitudes.at[core], amp),
            )
        )
    ]
    for at in range(64):
        chip_at = segment(core, sc[2] ^ (at // 8), sc[1] ^ (at % 8))
        source = recouple.at[core, pl.ds(pl.multiple_of(chip_at * seg, seg), seg)]
        copies.append(
            pltpu.make_async_copy(source, rows.at[at * seg : (at + 1) * seg], sems.at[at])
        )
    for copy in copies:
        copy.start()
    for copy in copies:
        copy.wait()


def load_call(sc, recouple, amplitudes, drive):
    _, n, half = amplitudes.shape
    return pl.pallas_call(
        load_kernel,
        grid_spec=pltpu.PrefetchScalarGridSpec(
            num_scalar_prefetch=1,
            grid=(1,),
            in_specs=[AWAY] * 3,
            out_specs=[WHOLE] * 4,
            scratch_shapes=[pltpu.SemaphoreType.DMA((67,))],
        ),
        out_shape=[VMEM((n, n), BF)] + [VMEM((n, half), BF)] * 3,
        compiler_params=params(1),
        cost_estimate=cost(0, 2 * n * n),
        name="load",
    )(sc, far(recouple), far(amplitudes), far(drive))


def spread(got, i, outs, columns):
    each = 8 // TILES
    seg = outs[0].shape[1]
    for j in range(each):
        piece = got[j * 8 * seg : (j + 1) * 8 * seg]
        outs[i * each + j][:, :, columns] = piece.reshape(8, seg, piece.shape[1])


def own_kernel(rows, amp, *refs):
    outs = refs[-8:]
    tile = rows.shape[0] // TILES
    for i in range(TILES):
        got = dot(rows[i * tile : (i + 1) * tile], amp[...]).astype(BF)
        spread(got, i, outs, slice(0, amp.shape[1]))


def own_call(rows, amp, *waits):
    n, half = amp.shape
    return pl.pallas_call(
        own_kernel,
        in_specs=[WHOLE, WHOLE] + [WAIT] * len(waits),
        out_specs=[WHOLE] * 8,
        out_shape=[VMEM((8, n // 64, 2 * half), BF)] * 8,
        compiler_params=params(4),
        cost_estimate=cost(2 * n * n * half, 2 * n * n),
        name="recoupled_own",
    )(held(rows), held(amp), *waits)


def other_kernel(rows, amp, *refs):
    outs = refs[-8:]
    n, half = amp.shape
    tile = n // TILES
    for i in range(TILES):
        got = dot(rows[i * tile : (i + 1) * tile], amp[...]).astype(BF)
        spread(got, i, outs, slice(half, 2 * half))


def other_call(rows, amp_other, begun, *waits):
    n, half = amp_other.shape
    return pl.pallas_call(
        other_kernel,
        in_specs=[WHOLE] * 10 + [WAIT] * len(waits),
        out_specs=[WHOLE] * 8,
        out_shape=[VMEM(begun[0].shape, BF)] * 8,
        input_output_aliases={2 + r: r for r in range(8)},
        compiler_params=params(4),
        cost_estimate=cost(2 * n * n * half, 4 * n * half),
        name="recoupled_other",
    )(held(rows), held(amp_other), *[held(block) for block in begun], *waits)


def coupling_kernel(sc, own, oth, *refs):
    out, sems = refs[-2:]
    half = own.shape[1]
    copies = []
    for part, ref in enumerate((own, oth)):
        for side in range(2):
            at = pl.ds(pl.multiple_of((sc[0] ^ side) * half, half), half)
            to = out.at[part * half : (part + 1) * half, side * half : (side + 1) * half]
            copies.append(pltpu.make_async_copy(ref.at[sc[0], :, at], to, sems.at[len(copies)]))
    for copy in copies:
        copy.start()
    for copy in copies:
        copy.wait()


def coupling_call(sc, own, oth, *waits):
    _, half, h = own.shape
    return pl.pallas_call(
        coupling_kernel,
        grid_spec=pltpu.PrefetchScalarGridSpec(
            num_scalar_prefetch=1,
            grid=(1,),
            in_specs=[AWAY, WAIT] + [WAIT] * len(waits),
            out_specs=WHOLE,
            scratch_shapes=[pltpu.SemaphoreType.DMA((4,))],
        ),
        out_shape=VMEM((h, h), BF),
        compiler_params=params(1),
        cost_estimate=cost(0, 4 * h * h),
        name="coupling",
    )(sc, far(own), oth, *waits)


def cycle_kernel(count, *refs):
    blocks, couplings, outs = refs[:count], refs[count : count + 8], refs[-count:]
    seg = blocks[0].shape[1]
    for k in range(8):
        lines = jnp.concatenate([block[k] for block in blocks], axis=0)
        got = dot(lines, couplings[k][...]).astype(BF)
        for r, out in enumerate(outs):
            out[k] = got[r * seg : (r + 1) * seg]


def cycle_call(blocks, couplings, *waits):
    count = len(blocks)
    _, rows, h = blocks[0].shape
    return pl.pallas_call(
        functools.partial(cycle_kernel, count),
        in_specs=[WHOLE] * (count + 8) + [WAIT] * len(waits),
        out_specs=[WHOLE] * count,
        out_shape=[VMEM(blocks[0].shape, BF)] * count,
        compiler_params=params(4),
        cost_estimate=cost(16 * count * rows * h * h, 32 * count * rows * h + 16 * h * h),
        name="cycle",
    )(*[held(b) for b in blocks], *[held(c) for c in couplings], *waits)


def ladder_kernel(tiles, sc, ladder_int, amp, amp_other, drive, drive_other, part, *refs):
    out, out_part = refs[-2:]
    core, half, tile = sc[0], amp.shape[1], amp.shape[0] // TILES
    for i in tiles:
        at = slice(i * tile, (i + 1) * tile)
        left = ladder_int[core, at]
        out[at, :half] = dot(left, amp[...]) + drive[core, at].astype(F32)
        out[at, half:] = dot(left, amp_other[...]) + drive_other[at].astype(F32)
        out_part[at, :] = jnp.broadcast_to(part[pl.ds(core, 1), at], (128, tile)).T


def ladder_call(tiles, begun, operands, *waits):
    n, half = operands[2].shape
    operands = operands[:1] + [held(a) for a in operands[1:]]
    return pl.pallas_call(
        functools.partial(ladder_kernel, tiles),
        grid_spec=pltpu.PrefetchScalarGridSpec(
            num_scalar_prefetch=1,
            grid=(1,),
            in_specs=[WHOLE] * (6 + len(begun)) + [WAIT] * len(waits),
            out_specs=[WHOLE, WHOLE],
        ),
        out_shape=[VMEM((n, 2 * half), F32), VMEM((n, 128), F32)],
        input_output_aliases={7 + i: i for i in range(len(begun))},
        compiler_params=params(4),
        cost_estimate=cost(n * n * half * len(tiles), 8 * n * half),
        name="ladder",
    )(*operands, *[held(array) for array in begun], *waits)


def gathered(blocks, lines, columns):
    rows = blocks[0].shape[0] * blocks[0].shape[1]
    for j, block in enumerate(blocks):
        got = block[:, :, columns]
        lines[j * rows : (j + 1) * rows, :] = got.reshape(rows, got.shape[2])


def folded_kernel(chosen, rows, ladder, *refs):
    blocks, (out, lines) = refs[: len(chosen)], refs[-2:]
    tile = rows.shape[1] // TILES
    gathered(blocks, lines, slice(0, lines.shape[1]))
    for i in range(TILES):
        at = slice(i * tile, (i + 1) * tile)
        out[at] = ladder[at] + folded(chosen, rows, at, lines)


def folded(chosen, rows, at, lines):
    each = rows.shape[0] // 8
    total = 0
    for j, r in enumerate(chosen):
        total += dot_rows(
            rows[r * each : (r + 1) * each, at], lines[j * each : (j + 1) * each, :]
        )
    return total


def folded_call(chosen, rows, returned, ladder, *waits):
    n, h = ladder.shape
    part = n * len(chosen) // 8
    return pl.pallas_call(
        functools.partial(folded_kernel, chosen),
        in_specs=[WHOLE] * (2 + len(chosen)) + [WAIT] * len(waits),
        out_specs=WHOLE,
        out_shape=VMEM(ladder.shape, F32),
        input_output_aliases={1: 0},
        scratch_shapes=[VMEM((part, h), BF)],
        compiler_params=params(8),
        cost_estimate=cost(2 * n * part * h, 6 * n * h),
        name="folded",
    )(held(rows), held(ladder), *[held(returned[r]) for r in chosen], *waits)


def final_kernel(chosen, side, sc, rows, ladder, part, hole, *refs):
    blocks, (out, lines) = refs[: len(chosen)], refs[-2:]
    core, i = sc[0], pl.program_id(0)
    tile, half = out.shape[-2:]
    cols = slice(side * half, (side + 1) * half)

    @pl.when(i == 0)
    def _():
        gathered(blocks, lines, cols)

    at = pl.ds(pl.multiple_of(i * tile, tile), tile)
    total = ladder[at, cols] + folded(chosen, rows, at, lines)
    got = (total / (part[at, :1] - hole[pl.ds(core, 1), :])).astype(BF)
    out[...] = got.reshape(out.shape)


def final_call(chosen, side, sc, rows, returned, ladder, part, hole, *waits):
    n, h = ladder.shape
    tile, half = n // TILES, h // 2
    if side == 0:
        out_spec = pl.BlockSpec((1, tile, half), lambda i, sc: (sc[0], i, 0))
    else:
        out_spec = pl.BlockSpec((tile, half), lambda i, sc: (i, 0))
    return pl.pallas_call(
        functools.partial(final_kernel, chosen, side),
        grid_spec=pltpu.PrefetchScalarGridSpec(
            num_scalar_prefetch=1,
            grid=(TILES,),
            in_specs=[WHOLE] * (4 + len(chosen)) + [WAIT] * len(waits),
            out_specs=out_spec,
            scratch_shapes=[VMEM((n * len(chosen) // 8, half), BF)],
        ),
        out_shape=pltpu.HBM((2, n, half), BF) if side == 0 else VMEM((n, half), BF),
        compiler_params=params(6),
        cost_estimate=cost(2 * n * n * half, 6 * n * half),
        name=("final_own", "final_other")[side],
    )(
        sc,
        held(rows),
        held(ladder),
        held(part),
        held(hole),
        *[held(returned[r]) for r in chosen],
        *waits,
    )


def place_kernel(sc, given, arrived, out, sem):
    copy = pltpu.make_async_copy(arrived, out.at[1 - sc[0]], sem)
    copy.start()
    copy.wait()


def place_call(sc, out, arrived):
    return pl.pallas_call(
        place_kernel,
        grid_spec=pltpu.PrefetchScalarGridSpec(
            num_scalar_prefetch=1,
            grid=(1,),
            in_specs=[AWAY, WAIT],
            out_specs=AWAY,
            scratch_shapes=[pltpu.SemaphoreType.DMA],
        ),
        out_shape=pltpu.HBM(out.shape, BF),
        input_output_aliases={1: 0},
        compiler_params=params(1),
        cost_estimate=cost(0, 2 * out.shape[1] * out.shape[2]),
        name="place",
    )(sc, far(out), arrived)


def local(amplitudes, recouple, ladder_int, cycle_coupling, drive, eps_part, eps_hole):
    core, here = lax.axis_index("dom"), lax.axis_index("chan")
    moved = kept = 0
    for weight in (16, 4, 1):
        place = (here // weight) % 4
        high, low = place // 2, ((place + 1) // 2) % 2
        moved = 2 * moved + jnp.where(core == 0, high, low)
        kept = 2 * kept + jnp.where(core == 0, low, high)
    sc = jnp.stack([core, kept, moved]).astype(jnp.int32)

    coupling_other = swap(cycle_coupling)
    hole_other = swap(eps_hole)
    rows, amp, amp_send, drive_send = load_call(sc, recouple, amplitudes, drive)
    c0 = coupling_call(sc, cycle_coupling, coupling_other, amp_send)
    amp_send, drive_send = tie([amp_send, drive_send], c0)
    amp_other, drive_other = swap(amp_send), swap(drive_send)

    c4, c2, c1 = over(c0, kept=4), over(c0, kept=2), over(c0, kept=1)
    begun = own_call(rows, amp, c0, hole_other)
    send = other_call(rows, amp_other, begun, drive_other)

    c4, c2, c1 = tie([c4, c2, c1], send[0])
    c6, c3, c5 = over(c4, kept=2), over(c2, kept=1), over(c1, kept=4)
    blocks = [send[0]] + [None] * 7
    for r in FIRST:
        blocks[r] = over(send[r], moved=r)
    operands = [sc, ladder_int, amp, amp_other, drive, drive_other, eps_part]
    begun = ladder_call((0, 1), (), operands, send[0])
    ladder, part = ladder_call((2, 3), begun, operands, *[blocks[r] for r in FIRST])

    c6, c3, c5, *rest = tie([c6, c3, c5] + [send[r] for r in THEN], ladder)
    c7 = over(c6, kept=1)
    for r, block in zip(THEN, rest):
        blocks[r] = over(block, moved=r)

    couplings = [c0, c1, c2, c3, c4, c5, c6, c7]
    returned = [None] * 8
    for group in BACK:
        for r, block in zip(group, cycle_call([blocks[r] for r in group], couplings)):
            returned[r] = over(block, moved=r) if r else block
    ladder = folded_call(EARLY, rows, returned, ladder)
    out_other = final_call(LATE, 1, sc, rows, returned, ladder, part, hole_other)
    out = final_call(LATE, 0, sc, rows, returned, ladder, part, eps_hole, out_other)
    return place_call(sc, out, swap(out_other))


def solution(mesh):
    placed = (
        P("chan", None, "dom"),
        P("chan", None, None),
        P("chan", None, None),
        P("chan", "dom", None),
        P("chan", None, "dom"),
        P("chan", None),
        P("chan", "dom"),
    )
    return jax.shard_map(
        local, mesh=mesh, in_specs=placed, out_specs=P("chan", None, "dom"), check_vma=False
    )
```

```python
import functools
import itertools

import jax
import jax.numpy as jnp
from jax import lax
from jax.experimental import pallas as pl
from jax.experimental.pallas import tpu as pltpu
from jax.sharding import PartitionSpec as P

RING = ((0, 0), (0, 1), (1, 1), (1, 0))
PLACE = {bits: at for at, bits in enumerate(RING)}
BF, F32 = jnp.bfloat16, jnp.float32
VMEM = pltpu.VMEM


def chip(bits):
    return (PLACE[bits[0]] * 4 + PLACE[bits[1]]) * 4 + PLACE[bits[2]]


HIGH = (1, 0, 1)


def bits_of(core, moved, kept):
    return [(m, k) if first ^ core else (k, m) for first, m, k in zip(HIGH, moved, kept)]


THREE = list(itertools.product((0, 1), repeat=3))
def flips(of_moved, of_kept):
    pairs = []
    for core, moved, kept in itertools.product(range(2), THREE, THREE):
        to = [m ^ f for m, f in zip(moved, THREE[of_moved])]
        at = [k ^ f for k, f in zip(kept, THREE[of_kept])]
        pairs.append(
            (
                chip(bits_of(core, moved, kept)) * 2 + core,
                chip(bits_of(core, to, at)) * 2 + core,
            )
        )
    return pairs


BOTH = ("chan", "dom")


def swap(array):
    return lax.ppermute(array, "dom", [(0, 1), (1, 0)])


def over(array, moved=0, kept=0):
    return lax.ppermute(array, BOTH, flips(moved, kept))


def segment(core, moved, kept):
    at = 0
    for first, shift in zip(HIGH, (2, 1, 0)):
        m, k = (moved >> shift) & 1, (kept >> shift) & 1
        at = at * 4 + 2 * jnp.where(core == 1 - first, m, k) + (m ^ k)
    return at


def dot(a, b):
    return jnp.dot(a, b, preferred_element_type=F32)


def dot_rows(a, b):
    return lax.dot_general(a, b, (((0,), (0,)), ((), ())), preferred_element_type=F32)


def params(mib):
    return pltpu.CompilerParams(vmem_limit_bytes=mib * 1024 * 1024)


def cost(flops, moved):
    return pl.CostEstimate(flops=flops, bytes_accessed=moved, transcendentals=0)


def held(array):
    return pltpu.with_memory_space_constraint(array, VMEM)


def far(array):
    return pltpu.with_memory_space_constraint(array, pltpu.HBM)


WHOLE = pl.BlockSpec(memory_space=VMEM)
AWAY = pl.BlockSpec(memory_space=pltpu.HBM)
WAIT = pl.BlockSpec(memory_space=pl.ANY)
TILES = 4
FIRST, THEN = (1, 3), (7, 5, 6, 2, 4)
BACK = (0, 7, 5, 3, 1), (6, 2, 4)
ORDER = BACK[0] + BACK[1]
EARLY, LATE = (range(5), range(5, 7)), range(7, 8)


def tie_kernel(*refs):
    pass


def tie(arrays, *waits):
    count = len(arrays)
    return pl.pallas_call(
        tie_kernel,
        in_specs=[WAIT] * (count + len(waits)),
        out_specs=[WAIT] * count,
        out_shape=[jax.ShapeDtypeStruct(a.shape, a.dtype) for a in arrays],
        input_output_aliases={i: i for i in range(count)},
        compiler_params=params(1),
        cost_estimate=cost(0, 0),
        name="tie",
    )(*arrays, *waits)


def cut_kernel(sc, amplitudes, drive, pair, sems):
    copies = [
        pltpu.make_async_copy(whole.at[1 - sc[0]], pair.at[i], sems.at[i])
        for i, whole in enumerate((amplitudes, drive))
    ]
    for copy in copies:
        copy.start()
    for copy in copies:
        copy.wait()


def cut_call(sc, amplitudes, drive):
    return pl.pallas_call(
        cut_kernel,
        grid_spec=pltpu.PrefetchScalarGridSpec(
            num_scalar_prefetch=1,
            grid=(1,),
            in_specs=[AWAY, AWAY],
            out_specs=WHOLE,
            scratch_shapes=[pltpu.SemaphoreType.DMA((2,))],
        ),
        out_shape=VMEM(amplitudes.shape, BF),
        compiler_params=params(1),
        cost_estimate=cost(0, 8 * amplitudes.shape[1] * amplitudes.shape[2]),
        name="cut",
    )(sc, far(amplitudes), far(drive))


def load_kernel(sc, recouple, amplitudes, *refs):
    rows, amp, sems = refs[-3:]
    core, seg = sc[0], rows.shape[0] // 64
    copies = [pltpu.make_async_copy(amplitudes.at[core], amp, sems.at[64])]
    for at in range(64):
        chip_at = segment(core, sc[2] ^ ORDER[at // 8], sc[1] ^ (at % 8))
        source = recouple.at[core, pl.ds(pl.multiple_of(chip_at * seg, seg), seg)]
        copies.append(
            pltpu.make_async_copy(source, rows.at[at * seg : (at + 1) * seg], sems.at[at])
        )
    for copy in copies:
        copy.start()
    for copy in copies:
        copy.wait()


def load_call(sc, recouple, amplitudes, *waits):
    _, n, half = amplitudes.shape
    return pl.pallas_call(
        load_kernel,
        grid_spec=pltpu.PrefetchScalarGridSpec(
            num_scalar_prefetch=1,
            grid=(1,),
            in_specs=[AWAY, AWAY] + [WAIT] * len(waits),
            out_specs=[WHOLE] * 2,
            scratch_shapes=[pltpu.SemaphoreType.DMA((65,))],
        ),
        out_shape=[VMEM((n, n), BF), VMEM((n, half), BF)],
        compiler_params=params(1),
        cost_estimate=cost(0, 4 * n * n),
        name="load",
    )(sc, far(recouple), far(amplitudes), *waits)


def spread(got, i, outs, columns):
    each = 8 // TILES
    seg = outs[0].shape[1]
    for j in range(each):
        piece = got[j * 8 * seg : (j + 1) * 8 * seg]
        outs[i * each + j][:, :, columns] = piece.reshape(8, seg, piece.shape[1])


def own_kernel(rows, amp, *refs):
    outs = refs[-8:]
    tile = rows.shape[0] // TILES
    for i in range(TILES):
        got = dot(rows[i * tile : (i + 1) * tile], amp[...]).astype(BF)
        spread(got, i, outs, slice(0, amp.shape[1]))


def own_call(rows, amp, *waits):
    n, half = amp.shape
    return pl.pallas_call(
        own_kernel,
        in_specs=[WHOLE, WHOLE] + [WAIT] * len(waits),
        out_specs=[WHOLE] * 8,
        out_shape=[VMEM((8, n // 64, 2 * half), BF)] * 8,
        compiler_params=params(4),
        cost_estimate=cost(2 * n * n * half, 2 * n * n),
        name="recoupled_own",
    )(held(rows), held(amp), *waits)


def other_kernel(rows, pair, *refs):
    outs = refs[-8:]
    _, n, half = pair.shape
    tile = n // TILES
    for i in range(TILES):
        got = dot(rows[i * tile : (i + 1) * tile], pair[0]).astype(BF)
        spread(got, i, outs, slice(half, 2 * half))


def other_call(rows, pair, begun, *waits):
    _, n, half = pair.shape
    return pl.pallas_call(
        other_kernel,
        in_specs=[WHOLE] * 10 + [WAIT] * len(waits),
        out_specs=[WHOLE] * 8,
        out_shape=[VMEM(begun[0].shape, BF)] * 8,
        input_output_aliases={2 + r: r for r in range(8)},
        compiler_params=params(4),
        cost_estimate=cost(2 * n * n * half, 4 * n * half),
        name="recoupled_other",
    )(held(rows), held(pair), *[held(block) for block in begun], *waits)


def coupling_kernel(sc, own, oth, *refs):
    out, sems = refs[-2:]
    half = own.shape[1]
    copies = []
    for part, ref in enumerate((own, oth)):
        for side in range(2):
            at = pl.ds(pl.multiple_of((sc[0] ^ side) * half, half), half)
            to = out.at[part * half : (part + 1) * half, side * half : (side + 1) * half]
            copies.append(pltpu.make_async_copy(ref.at[sc[0], :, at], to, sems.at[len(copies)]))
    for copy in copies:
        copy.start()
    for copy in copies:
        copy.wait()


def coupling_call(sc, own, oth, *waits):
    _, half, h = own.shape
    return pl.pallas_call(
        coupling_kernel,
        grid_spec=pltpu.PrefetchScalarGridSpec(
            num_scalar_prefetch=1,
            grid=(1,),
            in_specs=[AWAY, WAIT] + [WAIT] * len(waits),
            out_specs=WHOLE,
            scratch_shapes=[pltpu.SemaphoreType.DMA((4,))],
        ),
        out_shape=VMEM((h, h), BF),
        compiler_params=params(1),
        cost_estimate=cost(0, 4 * h * h),
        name="coupling",
    )(sc, far(own), oth, *waits)


def cycle_kernel(count, *refs):
    blocks, couplings, outs = refs[:count], refs[count : count + 8], refs[-count:]
    seg = blocks[0].shape[1]
    for k in range(8):
        lines = jnp.concatenate([block[k] for block in blocks], axis=0)
        got = dot(lines, couplings[k][...]).astype(BF)
        for r, out in enumerate(outs):
            out[k] = got[r * seg : (r + 1) * seg]


def cycle_call(blocks, couplings, *waits):
    count = len(blocks)
    _, rows, h = blocks[0].shape
    return pl.pallas_call(
        functools.partial(cycle_kernel, count),
        in_specs=[WHOLE] * (count + 8) + [WAIT] * len(waits),
        out_specs=[WHOLE] * count,
        out_shape=[VMEM(blocks[0].shape, BF)] * count,
        compiler_params=params(4),
        cost_estimate=cost(16 * count * rows * h * h, 32 * count * rows * h + 16 * h * h),
        name="cycle",
    )(*[held(b) for b in blocks], *[held(c) for c in couplings], *waits)


def ladder_kernel(tiles, sc, ladder_int, amp, drive, pair, part, *refs):
    out, out_part = refs[-2:]
    core, half, tile = sc[0], amp.shape[1], amp.shape[0] // TILES
    for i in tiles:
        at = slice(i * tile, (i + 1) * tile)
        left = ladder_int[core, at]
        out[at, :half] = dot(left, amp[...]) + drive[core, at].astype(F32)
        out[at, half:] = dot(left, pair[0]) + pair[1, at].astype(F32)
        out_part[at, :] = jnp.broadcast_to(part[pl.ds(core, 1), at], (128, tile)).T


def ladder_call(tiles, begun, operands, *waits):
    n, half = operands[2].shape
    operands = operands[:1] + [held(a) for a in operands[1:]]
    return pl.pallas_call(
        functools.partial(ladder_kernel, tiles),
        grid_spec=pltpu.PrefetchScalarGridSpec(
            num_scalar_prefetch=1,
            grid=(1,),
            in_specs=[WHOLE] * (5 + len(begun)) + [WAIT] * len(waits),
            out_specs=[WHOLE, WHOLE],
        ),
        out_shape=[VMEM((n, 2 * half), F32), VMEM((n, 128), F32)],
        input_output_aliases={6 + i: i for i in range(len(begun))},
        compiler_params=params(4),
        cost_estimate=cost(n * n * half * len(tiles), 8 * n * half),
        name="ladder",
    )(*operands, *[held(array) for array in begun], *waits)


def gathered(blocks, lines, columns):
    rows = blocks[0].shape[0] * blocks[0].shape[1]
    for j, block in enumerate(blocks):
        got = block[:, :, columns]
        lines[j * rows : (j + 1) * rows, :] = got.reshape(rows, got.shape[2])


def folded_kernel(chosen, rows, ladder, *refs):
    blocks, (out, lines) = refs[: len(chosen)], refs[-2:]
    tile = rows.shape[1] // TILES
    gathered(blocks, lines, slice(0, lines.shape[1]))
    for i in range(TILES):
        at = slice(i * tile, (i + 1) * tile)
        out[at] = ladder[at] + folded(chosen, rows, at, lines)


def folded(chosen, rows, at, lines):
    each = rows.shape[0] // 8
    return dot_rows(rows[chosen[0] * each : (chosen[-1] + 1) * each, at], lines[...])


def folded_call(chosen, rows, returned, ladder, *waits):
    n, h = ladder.shape
    part = n * len(chosen) // 8
    return pl.pallas_call(
        functools.partial(folded_kernel, chosen),
        in_specs=[WHOLE] * (2 + len(chosen)) + [WAIT] * len(waits),
        out_specs=WHOLE,
        out_shape=VMEM(ladder.shape, F32),
        input_output_aliases={1: 0},
        scratch_shapes=[VMEM((part, h), BF)],
        compiler_params=params(8),
        cost_estimate=cost(2 * n * part * h, 6 * n * h),
        name="folded",
    )(held(rows), held(ladder), *[held(returned[r]) for r in chosen], *waits)


def final_kernel(chosen, side, sc, rows, ladder, part, hole, *refs):
    blocks, (out, lines, made, sems) = refs[: len(chosen)], refs[-4:]
    n, half = lines.shape[0] * 8 // len(chosen), lines.shape[1]
    tile = n // TILES
    cols = slice(side * half, (side + 1) * half)
    gathered(blocks, lines, cols)
    copies = []
    for i in range(TILES):
        at = slice(i * tile, (i + 1) * tile)
        total = ladder[at, cols] + folded(chosen, rows, at, lines)
        got = (total / (part[at, :1] - hole[pl.ds(sc[0], 1), :])).astype(BF)
        if side == 1:
            out[at] = got
        else:
            made[at] = got
            copies.append(
                pltpu.make_async_copy(made.at[at], out.at[sc[0], at], sems.at[i])
            )
            copies[-1].start()
    for copy in copies:
        copy.wait()


def final_call(chosen, side, sc, rows, returned, ladder, part, hole, *waits):
    n, h = ladder.shape
    half = h // 2
    return pl.pallas_call(
        functools.partial(final_kernel, chosen, side),
        grid_spec=pltpu.PrefetchScalarGridSpec(
            num_scalar_prefetch=1,
            grid=(1,),
            in_specs=[WHOLE] * (4 + len(chosen)) + [WAIT] * len(waits),
            out_specs=WHOLE if side else AWAY,
            scratch_shapes=[
                VMEM((n * len(chosen) // 8, half), BF),
                VMEM((n, half), BF),
                pltpu.SemaphoreType.DMA((TILES,)),
            ],
        ),
        out_shape=VMEM((n, half), BF) if side else pltpu.HBM((2, n, half), BF),
        compiler_params=params(6),
        cost_estimate=cost(2 * n * n * half, 6 * n * half),
        name=("final_own", "final_other")[side],
    )(
        sc,
        held(rows),
        held(ladder),
        held(part),
        held(hole),
        *[held(returned[r]) for r in chosen],
        *waits,
    )


def place_kernel(sc, arrived, given, out, sems):
    each = arrived.shape[0] // TILES
    copies = []
    for i in range(TILES):
        at = slice(i * each, (i + 1) * each)
        copies.append(
            pltpu.make_async_copy(arrived.at[at], out.at[1 - sc[0], at], sems.at[i])
        )
    for copy in copies:
        copy.start()
    for copy in copies:
        copy.wait()


def place_call(sc, arrived, out):
    n, half = arrived.shape
    return pl.pallas_call(
        place_kernel,
        grid_spec=pltpu.PrefetchScalarGridSpec(
            num_scalar_prefetch=1,
            grid=(1,),
            in_specs=[WHOLE, AWAY],
            out_specs=AWAY,
            scratch_shapes=[pltpu.SemaphoreType.DMA((TILES,))],
        ),
        out_shape=pltpu.HBM((2, n, half), BF),
        input_output_aliases={2: 0},
        compiler_params=params(1),
        cost_estimate=cost(0, 4 * n * half),
        name="place",
    )(sc, held(arrived), far(out))


def local(amplitudes, recouple, ladder_int, cycle_coupling, drive, eps_part, eps_hole):
    core, here = lax.axis_index("dom"), lax.axis_index("chan")
    moved = kept = 0
    for first, weight in zip(HIGH, (16, 4, 1)):
        place = (here // weight) % 4
        high, low = place // 2, ((place + 1) // 2) % 2
        moved = 2 * moved + jnp.where(core == 1 - first, high, low)
        kept = 2 * kept + jnp.where(core == 1 - first, low, high)
    sc = jnp.stack([core, kept, moved]).astype(jnp.int32)

    coupling_other = swap(cycle_coupling)
    hole_other = swap(eps_hole)
    pair = cut_call(sc, amplitudes, drive)
    c0 = coupling_call(sc, cycle_coupling, coupling_other, pair, hole_other)
    (pair,) = tie([pair], c0)
    pair = swap(pair)

    c4, c2, c1 = over(c0, kept=4), over(c0, kept=2), over(c0, kept=1)
    rows, amp = load_call(sc, recouple, amplitudes, c0)

    begun = own_call(rows, amp)
    c4, c2, c1 = tie([c4, c2, c1], begun[0])
    c6, c3, c5 = over(c4, kept=2), over(c2, kept=1), over(c1, kept=4)
    send = dict(zip(ORDER, other_call(rows, pair, begun)))

    blocks = {0: send[0]}
    for r in FIRST:
        blocks[r] = over(send[r], moved=r)
    operands = [sc, ladder_int, amp, drive, pair, eps_part]
    ladder = ladder_call((0,), (), operands)

    c6, c3, c5, *rest = tie(
        [c6, c3, c5] + [send[r] for r in THEN], ladder[0], blocks[FIRST[0]]
    )
    c7 = over(c6, kept=1)
    for r, block in zip(THEN, rest):
        blocks[r] = over(block, moved=r)
    ladder, part = ladder_call((1, 2, 3), ladder, operands)

    couplings = [c0, c1, c2, c3, c4, c5, c6, c7]
    returned = []
    for group in BACK:
        cycled = cycle_call([blocks[r] for r in group], couplings, ladder)
        returned += [over(block, moved=r) if r else block for r, block in zip(group, cycled)]
    for group in EARLY:
        ladder = folded_call(group, rows, returned, ladder)
    out_other = final_call(LATE, 1, sc, rows, returned, ladder, part, hole_other)
    out = final_call(LATE, 0, sc, rows, returned, ladder, part, eps_hole, out_other)
    return place_call(sc, swap(out_other), out)


def solution(mesh):
    placed = (
        P("chan", None, "dom"),
        P("chan", None, None),
        P("chan", None, None),
        P("chan", "dom", None),
        P("chan", None, "dom"),
        P("chan", None),
        P("chan", "dom"),
    )
    return jax.shard_map(
        local, mesh=mesh, in_specs=placed, out_specs=P("chan", None, "dom"), check_vma=False
    )
```

```python
import functools
import itertools

import jax
import jax.numpy as jnp
from jax import lax
from jax.experimental import pallas as pl
from jax.experimental.pallas import tpu as pltpu
from jax.sharding import PartitionSpec as P

RING = ((0, 0), (0, 1), (1, 1), (1, 0))
PLACE = {bits: at for at, bits in enumerate(RING)}
BF, F32 = jnp.bfloat16, jnp.float32
VMEM = pltpu.VMEM


def chip(bits):
    return (PLACE[bits[0]] * 4 + PLACE[bits[1]]) * 4 + PLACE[bits[2]]


HIGH = (0, 0, 0)


def bits_of(core, moved, kept):
    return [(m, k) if first ^ core else (k, m) for first, m, k in zip(HIGH, moved, kept)]


THREE = list(itertools.product((0, 1), repeat=3))
def flips(of_moved, of_kept):
    pairs = []
    for core, moved, kept in itertools.product(range(2), THREE, THREE):
        to = [m ^ f for m, f in zip(moved, THREE[of_moved])]
        at = [k ^ f for k, f in zip(kept, THREE[of_kept])]
        pairs.append(
            (
                chip(bits_of(core, moved, kept)) * 2 + core,
                chip(bits_of(core, to, at)) * 2 + core,
            )
        )
    return pairs


BOTH = ("chan", "dom")


def swap(array):
    return lax.ppermute(array, "dom", [(0, 1), (1, 0)])


def over(array, moved=0, kept=0):
    return lax.ppermute(array, BOTH, flips(moved, kept))


def segment(core, moved, kept):
    at = 0
    for first, shift in zip(HIGH, (2, 1, 0)):
        m, k = (moved >> shift) & 1, (kept >> shift) & 1
        at = at * 4 + 2 * jnp.where(core == 1 - first, m, k) + (m ^ k)
    return at


def dot(a, b):
    return jnp.dot(a, b, preferred_element_type=F32)


def dot_rows(a, b):
    return lax.dot_general(a, b, (((0,), (0,)), ((), ())), preferred_element_type=F32)


def params(mib):
    return pltpu.CompilerParams(vmem_limit_bytes=mib * 1024 * 1024)


def cost(flops, moved):
    return pl.CostEstimate(flops=flops, bytes_accessed=moved, transcendentals=0)


def held(array):
    return pltpu.with_memory_space_constraint(array, VMEM)


def far(array):
    return pltpu.with_memory_space_constraint(array, pltpu.HBM)


WHOLE = pl.BlockSpec(memory_space=VMEM)
AWAY = pl.BlockSpec(memory_space=pltpu.HBM)
WAIT = pl.BlockSpec(memory_space=pl.ANY)
TILES = 4
FIRST, THEN = (1, 7), (2, 4, 3, 5, 6)
BACK = (0, 7, 1, 2, 4), (3, 5, 6)
ORDER = BACK[0] + BACK[1]
EARLY, LATE = (range(2), range(2, 5), range(5, 6)), range(6, 8)


def tie_kernel(*refs):
    pass


def tie(arrays, *waits):
    count = len(arrays)
    return pl.pallas_call(
        tie_kernel,
        in_specs=[WAIT] * (count + len(waits)),
        out_specs=[WAIT] * count,
        out_shape=[jax.ShapeDtypeStruct(a.shape, a.dtype) for a in arrays],
        input_output_aliases={i: i for i in range(count)},
        compiler_params=params(1),
        cost_estimate=cost(0, 0),
        name="tie",
    )(*arrays, *waits)


def cut_kernel(sc, amplitudes, drive, pair, sems):
    copies = [
        pltpu.make_async_copy(whole.at[1 - sc[0]], pair.at[i], sems.at[i])
        for i, whole in enumerate((amplitudes, drive))
    ]
    for copy in copies:
        copy.start()
    for copy in copies:
        copy.wait()


def cut_call(sc, amplitudes, drive):
    return pl.pallas_call(
        cut_kernel,
        grid_spec=pltpu.PrefetchScalarGridSpec(
            num_scalar_prefetch=1,
            grid=(1,),
            in_specs=[AWAY, AWAY],
            out_specs=WHOLE,
            scratch_shapes=[pltpu.SemaphoreType.DMA((2,))],
        ),
        out_shape=VMEM(amplitudes.shape, BF),
        compiler_params=params(1),
        cost_estimate=cost(0, 8 * amplitudes.shape[1] * amplitudes.shape[2]),
        name="cut",
    )(sc, far(amplitudes), far(drive))


def load_kernel(sc, recouple, amplitudes, *refs):
    rows, amp, sems = refs[-3:]
    core, seg = sc[0], rows.shape[0] // 64
    copies = [pltpu.make_async_copy(amplitudes.at[core], amp, sems.at[64])]
    for at in range(64):
        chip_at = segment(core, sc[2] ^ ORDER[at // 8], sc[1] ^ (at % 8))
        source = recouple.at[core, pl.ds(pl.multiple_of(chip_at * seg, seg), seg)]
        copies.append(
            pltpu.make_async_copy(source, rows.at[at * seg : (at + 1) * seg], sems.at[at])
        )
    for copy in copies:
        copy.start()
    for copy in copies:
        copy.wait()


def load_call(sc, recouple, amplitudes, *waits):
    _, n, half = amplitudes.shape
    return pl.pallas_call(
        load_kernel,
        grid_spec=pltpu.PrefetchScalarGridSpec(
            num_scalar_prefetch=1,
            grid=(1,),
            in_specs=[AWAY, AWAY] + [WAIT] * len(waits),
            out_specs=[WHOLE] * 2,
            scratch_shapes=[pltpu.SemaphoreType.DMA((65,))],
        ),
        out_shape=[VMEM((n, n), BF), VMEM((n, half), BF)],
        compiler_params=params(1),
        cost_estimate=cost(0, 4 * n * n),
        name="load",
    )(sc, far(recouple), far(amplitudes), *waits)


def spread(got, i, outs, columns):
    each = 8 // TILES
    seg = outs[0].shape[1]
    for j in range(each):
        piece = got[j * 8 * seg : (j + 1) * 8 * seg]
        outs[i * each + j][:, :, columns] = piece.reshape(8, seg, piece.shape[1])


def own_kernel(rows, amp, *refs):
    outs = refs[-8:]
    tile = rows.shape[0] // TILES
    for i in range(TILES):
        got = dot(rows[i * tile : (i + 1) * tile], amp[...]).astype(BF)
        spread(got, i, outs, slice(0, amp.shape[1]))


def own_call(rows, amp, *waits):
    n, half = amp.shape
    return pl.pallas_call(
        own_kernel,
        in_specs=[WHOLE, WHOLE] + [WAIT] * len(waits),
        out_specs=[WHOLE] * 8,
        out_shape=[VMEM((8, n // 64, 2 * half), BF)] * 8,
        compiler_params=params(4),
        cost_estimate=cost(2 * n * n * half, 2 * n * n),
        name="recoupled_own",
    )(held(rows), held(amp), *waits)


def other_kernel(rows, pair, *refs):
    outs = refs[-8:]
    _, n, half = pair.shape
    tile = n // TILES
    for i in range(TILES):
        got = dot(rows[i * tile : (i + 1) * tile], pair[0]).astype(BF)
        spread(got, i, outs, slice(half, 2 * half))


def other_call(rows, pair, begun, *waits):
    _, n, half = pair.shape
    return pl.pallas_call(
        other_kernel,
        in_specs=[WHOLE] * 10 + [WAIT] * len(waits),
        out_specs=[WHOLE] * 8,
        out_shape=[VMEM(begun[0].shape, BF)] * 8,
        input_output_aliases={2 + r: r for r in range(8)},
        compiler_params=params(4),
        cost_estimate=cost(2 * n * n * half, 4 * n * half),
        name="recoupled_other",
    )(held(rows), held(pair), *[held(block) for block in begun], *waits)


def coupling_kernel(sc, own, oth, *refs):
    out, sems = refs[-2:]
    half = own.shape[1]
    copies = []
    for part, ref in enumerate((own, oth)):
        for side in range(2):
            at = pl.ds(pl.multiple_of((sc[0] ^ side) * half, half), half)
            to = out.at[part * half : (part + 1) * half, side * half : (side + 1) * half]
            copies.append(pltpu.make_async_copy(ref.at[sc[0], :, at], to, sems.at[len(copies)]))
    for copy in copies:
        copy.start()
    for copy in copies:
        copy.wait()


def coupling_call(sc, own, oth, *waits):
    _, half, h = own.shape
    return pl.pallas_call(
        coupling_kernel,
        grid_spec=pltpu.PrefetchScalarGridSpec(
            num_scalar_prefetch=1,
            grid=(1,),
            in_specs=[AWAY, WAIT] + [WAIT] * len(waits),
            out_specs=WHOLE,
            scratch_shapes=[pltpu.SemaphoreType.DMA((4,))],
        ),
        out_shape=VMEM((h, h), BF),
        compiler_params=params(1),
        cost_estimate=cost(0, 4 * h * h),
        name="coupling",
    )(sc, far(own), oth, *waits)


def cycle_kernel(count, *refs):
    blocks, couplings, outs = refs[:count], refs[count : count + 8], refs[-count:]
    seg = blocks[0].shape[1]
    for k in range(8):
        lines = jnp.concatenate([block[k] for block in blocks], axis=0)
        got = dot(lines, couplings[k][...]).astype(BF)
        for r, out in enumerate(outs):
            out[k] = got[r * seg : (r + 1) * seg]


def cycle_call(blocks, couplings, *waits):
    count = len(blocks)
    _, rows, h = blocks[0].shape
    return pl.pallas_call(
        functools.partial(cycle_kernel, count),
        in_specs=[WHOLE] * (count + 8) + [WAIT] * len(waits),
        out_specs=[WHOLE] * count,
        out_shape=[VMEM(blocks[0].shape, BF)] * count,
        compiler_params=params(4),
        cost_estimate=cost(16 * count * rows * h * h, 32 * count * rows * h + 16 * h * h),
        name="cycle",
    )(*[held(b) for b in blocks], *[held(c) for c in couplings], *waits)


def ladder_kernel(tiles, sc, ladder_int, amp, drive, pair, part, *refs):
    out, out_part = refs[-2:]
    core, half, tile = sc[0], amp.shape[1], amp.shape[0] // TILES
    for i in tiles:
        at = slice(i * tile, (i + 1) * tile)
        left = ladder_int[core, at]
        out[at, :half] = dot(left, amp[...]) + drive[core, at].astype(F32)
        out[at, half:] = dot(left, pair[0]) + pair[1, at].astype(F32)
        out_part[at, :] = jnp.broadcast_to(part[pl.ds(core, 1), at], (128, tile)).T


def ladder_call(tiles, begun, operands, *waits):
    n, half = operands[2].shape
    operands = operands[:1] + [held(a) for a in operands[1:]]
    return pl.pallas_call(
        functools.partial(ladder_kernel, tiles),
        grid_spec=pltpu.PrefetchScalarGridSpec(
            num_scalar_prefetch=1,
            grid=(1,),
            in_specs=[WHOLE] * (5 + len(begun)) + [WAIT] * len(waits),
            out_specs=[WHOLE, WHOLE],
        ),
        out_shape=[VMEM((n, 2 * half), F32), VMEM((n, 128), F32)],
        input_output_aliases={6 + i: i for i in range(len(begun))},
        compiler_params=params(4),
        cost_estimate=cost(n * n * half * len(tiles), 8 * n * half),
        name="ladder",
    )(*operands, *[held(array) for array in begun], *waits)


def gathered(blocks, lines, columns):
    rows = blocks[0].shape[0] * blocks[0].shape[1]
    for j, block in enumerate(blocks):
        got = block[:, :, columns]
        lines[j * rows : (j + 1) * rows, :] = got.reshape(rows, got.shape[2])


def folded_kernel(chosen, rows, ladder, *refs):
    blocks, (out, lines) = refs[: len(chosen)], refs[-2:]
    tile = rows.shape[1] // TILES
    gathered(blocks, lines, slice(0, lines.shape[1]))
    for i in range(TILES):
        at = slice(i * tile, (i + 1) * tile)
        out[at] = ladder[at] + folded(chosen, rows, at, lines)


def folded(chosen, rows, at, lines):
    each = rows.shape[0] // 8
    return dot_rows(rows[chosen[0] * each : (chosen[-1] + 1) * each, at], lines[...])


def folded_call(chosen, rows, returned, ladder, *waits):
    n, h = ladder.shape
    part = n * len(chosen) // 8
    return pl.pallas_call(
        functools.partial(folded_kernel, chosen),
        in_specs=[WHOLE] * (2 + len(chosen)) + [WAIT] * len(waits),
        out_specs=WHOLE,
        out_shape=VMEM(ladder.shape, F32),
        input_output_aliases={1: 0},
        scratch_shapes=[VMEM((part, h), BF)],
        compiler_params=params(8),
        cost_estimate=cost(2 * n * part * h, 6 * n * h),
        name="folded",
    )(held(rows), held(ladder), *[held(returned[r]) for r in chosen], *waits)


def final_kernel(chosen, side, sc, rows, ladder, part, hole, *refs):
    blocks, (out, lines, made, sems) = refs[: len(chosen)], refs[-4:]
    n, half = lines.shape[0] * 8 // len(chosen), lines.shape[1]
    tile = n // TILES
    cols = slice(side * half, (side + 1) * half)
    gathered(blocks, lines, cols)
    copies = []
    for i in range(TILES):
        at = slice(i * tile, (i + 1) * tile)
        total = ladder[at, cols] + folded(chosen, rows, at, lines)
        got = (total / (part[at, :1] - hole[pl.ds(sc[0], 1), :])).astype(BF)
        if side == 1:
            out[at] = got
        else:
            made[at] = got
            copies.append(
                pltpu.make_async_copy(made.at[at], out.at[sc[0], at], sems.at[i])
            )
            copies[-1].start()
    for copy in copies:
        copy.wait()


def final_call(chosen, side, sc, rows, returned, ladder, part, hole, *waits):
    n, h = ladder.shape
    half = h // 2
    return pl.pallas_call(
        functools.partial(final_kernel, chosen, side),
        grid_spec=pltpu.PrefetchScalarGridSpec(
            num_scalar_prefetch=1,
            grid=(1,),
            in_specs=[WHOLE] * (4 + len(chosen)) + [WAIT] * len(waits),
            out_specs=WHOLE if side else AWAY,
            scratch_shapes=[
                VMEM((n * len(chosen) // 8, half), BF),
                VMEM((n, half), BF),
                pltpu.SemaphoreType.DMA((TILES,)),
            ],
        ),
        out_shape=VMEM((n, half), BF) if side else pltpu.HBM((2, n, half), BF),
        compiler_params=params(6),
        cost_estimate=cost(2 * n * n * half, 6 * n * half),
        name=("final_own", "final_other")[side],
    )(
        sc,
        held(rows),
        held(ladder),
        held(part),
        held(hole),
        *[held(returned[r]) for r in chosen],
        *waits,
    )


def place_kernel(sc, arrived, given, out, sems):
    each = arrived.shape[0] // TILES
    copies = []
    for i in range(TILES):
        at = slice(i * each, (i + 1) * each)
        copies.append(
            pltpu.make_async_copy(arrived.at[at], out.at[1 - sc[0], at], sems.at[i])
        )
    for copy in copies:
        copy.start()
    for copy in copies:
        copy.wait()


def place_call(sc, arrived, out):
    n, half = arrived.shape
    return pl.pallas_call(
        place_kernel,
        grid_spec=pltpu.PrefetchScalarGridSpec(
            num_scalar_prefetch=1,
            grid=(1,),
            in_specs=[WHOLE, AWAY],
            out_specs=AWAY,
            scratch_shapes=[pltpu.SemaphoreType.DMA((TILES,))],
        ),
        out_shape=pltpu.HBM((2, n, half), BF),
        input_output_aliases={2: 0},
        compiler_params=params(1),
        cost_estimate=cost(0, 4 * n * half),
        name="place",
    )(sc, held(arrived), far(out))


def local(amplitudes, recouple, ladder_int, cycle_coupling, drive, eps_part, eps_hole):
    core, here = lax.axis_index("dom"), lax.axis_index("chan")
    moved = kept = 0
    for first, weight in zip(HIGH, (16, 4, 1)):
        place = (here // weight) % 4
        high, low = place // 2, ((place + 1) // 2) % 2
        moved = 2 * moved + jnp.where(core == 1 - first, high, low)
        kept = 2 * kept + jnp.where(core == 1 - first, low, high)
    sc = jnp.stack([core, kept, moved]).astype(jnp.int32)

    coupling_other = swap(cycle_coupling)
    hole_other = swap(eps_hole)
    pair = cut_call(sc, amplitudes, drive)
    c0 = coupling_call(sc, cycle_coupling, coupling_other, pair, hole_other)
    (pair,) = tie([pair], c0)
    pair = swap(pair)

    c4, c2, c1 = over(c0, kept=4), over(c0, kept=2), over(c0, kept=1)
    rows, amp = load_call(sc, recouple, amplitudes, c0)

    begun = own_call(rows, amp)
    c4, c2, c1 = tie([c4, c2, c1], begun[0])
    c6, c3, c5 = over(c4, kept=2), over(c2, kept=1), over(c1, kept=4)
    send = dict(zip(ORDER, other_call(rows, pair, begun)))

    blocks = {0: send[0]}
    for r in FIRST:
        blocks[r] = over(send[r], moved=r)
    operands = [sc, ladder_int, amp, drive, pair, eps_part]
    ladder = ladder_call((0,), (), operands)

    c6, c3, c5, *rest = tie(
        [c6, c3, c5] + [send[r] for r in THEN], ladder[0], blocks[FIRST[0]]
    )
    c7 = over(c6, kept=1)
    for r, block in zip(THEN, rest):
        blocks[r] = over(block, moved=r)
    ladder, part = ladder_call((1, 2, 3), ladder, operands)

    couplings = [c0, c1, c2, c3, c4, c5, c6, c7]
    returned = []
    for group in BACK:
        cycled = cycle_call([blocks[r] for r in group], couplings, ladder)
        returned += [over(block, moved=r) if r else block for r, block in zip(group, cycled)]
    for group in EARLY:
        ladder = folded_call(group, rows, returned, ladder)
    out_other = final_call(LATE, 1, sc, rows, returned, ladder, part, hole_other)
    out = final_call(LATE, 0, sc, rows, returned, ladder, part, eps_hole, out_other)
    return place_call(sc, swap(out_other), out)


def solution(mesh):
    placed = (
        P("chan", None, "dom"),
        P("chan", None, None),
        P("chan", None, None),
        P("chan", "dom", None),
        P("chan", None, "dom"),
        P("chan", None),
        P("chan", "dom"),
    )
    return jax.shard_map(
        local, mesh=mesh, in_specs=placed, out_specs=P("chan", None, "dom"), check_vma=False
    )
```

```python
import functools
import itertools

import jax
import jax.numpy as jnp
from jax import lax
from jax.experimental import pallas as pl
from jax.experimental.pallas import tpu as pltpu
from jax.sharding import PartitionSpec as P

RING = ((0, 0), (0, 1), (1, 1), (1, 0))
PLACE = {bits: at for at, bits in enumerate(RING)}
BF, F32 = jnp.bfloat16, jnp.float32
VMEM = pltpu.VMEM


def chip(bits):
    return (PLACE[bits[0]] * 4 + PLACE[bits[1]]) * 4 + PLACE[bits[2]]


HIGH = (0, 0, 0)


def bits_of(core, moved, kept):
    return [(m, k) if first ^ core else (k, m) for first, m, k in zip(HIGH, moved, kept)]


THREE = list(itertools.product((0, 1), repeat=3))
def flips(of_moved, of_kept):
    pairs = []
    for core, moved, kept in itertools.product(range(2), THREE, THREE):
        to = [m ^ f for m, f in zip(moved, THREE[of_moved])]
        at = [k ^ f for k, f in zip(kept, THREE[of_kept])]
        pairs.append(
            (
                chip(bits_of(core, moved, kept)) * 2 + core,
                chip(bits_of(core, to, at)) * 2 + core,
            )
        )
    return pairs


BOTH = ("chan", "dom")


def swap(array):
    return lax.ppermute(array, "dom", [(0, 1), (1, 0)])


def over(array, moved=0, kept=0):
    return lax.ppermute(array, BOTH, flips(moved, kept))


def segment(core, moved, kept):
    at = 0
    for first, shift in zip(HIGH, (2, 1, 0)):
        m, k = (moved >> shift) & 1, (kept >> shift) & 1
        at = at * 4 + 2 * jnp.where(core == 1 - first, m, k) + (m ^ k)
    return at


def dot(a, b):
    return jnp.dot(a, b, preferred_element_type=F32)


def dot_rows(a, b):
    return lax.dot_general(a, b, (((0,), (0,)), ((), ())), preferred_element_type=F32)


def params(mib):
    return pltpu.CompilerParams(vmem_limit_bytes=mib * 1024 * 1024)


def cost(flops, moved):
    return pl.CostEstimate(flops=flops, bytes_accessed=moved, transcendentals=0)


def held(array):
    return pltpu.with_memory_space_constraint(array, VMEM)


def far(array):
    return pltpu.with_memory_space_constraint(array, pltpu.HBM)


WHOLE = pl.BlockSpec(memory_space=VMEM)
AWAY = pl.BlockSpec(memory_space=pltpu.HBM)
WAIT = pl.BlockSpec(memory_space=pl.ANY)
TILES = 4
FIRST, THEN = (1, 7), (2, 4, 3, 5, 6)
BACK = (0, 1, 2, 4, 7), (3, 5, 6)
ORDER = BACK[0] + BACK[1]
EARLY, LATE = (range(2), range(2, 5), range(5, 6)), range(6, 8)


def tie_kernel(*refs):
    pass


def tie(arrays, *waits):
    count = len(arrays)
    return pl.pallas_call(
        tie_kernel,
        in_specs=[WAIT] * (count + len(waits)),
        out_specs=[WAIT] * count,
        out_shape=[jax.ShapeDtypeStruct(a.shape, a.dtype) for a in arrays],
        input_output_aliases={i: i for i in range(count)},
        compiler_params=params(1),
        cost_estimate=cost(0, 0),
        name="tie",
    )(*arrays, *waits)


def cut_kernel(sc, amplitudes, drive, pair, sems):
    copies = [
        pltpu.make_async_copy(whole.at[1 - sc[0]], pair.at[i], sems.at[i])
        for i, whole in enumerate((amplitudes, drive))
    ]
    for copy in copies:
        copy.start()
    for copy in copies:
        copy.wait()


def cut_call(sc, amplitudes, drive):
    return pl.pallas_call(
        cut_kernel,
        grid_spec=pltpu.PrefetchScalarGridSpec(
            num_scalar_prefetch=1,
            grid=(1,),
            in_specs=[AWAY, AWAY],
            out_specs=WHOLE,
            scratch_shapes=[pltpu.SemaphoreType.DMA((2,))],
        ),
        out_shape=VMEM(amplitudes.shape, BF),
        compiler_params=params(1),
        cost_estimate=cost(0, 8 * amplitudes.shape[1] * amplitudes.shape[2]),
        name="cut",
    )(sc, far(amplitudes), far(drive))


def load_kernel(sc, recouple, amplitudes, *refs):
    rows, amp, sems = refs[-3:]
    core, seg = sc[0], rows.shape[0] // 64
    copies = [pltpu.make_async_copy(amplitudes.at[core], amp, sems.at[64])]
    for at in range(64):
        chip_at = segment(core, sc[2] ^ ORDER[at // 8], sc[1] ^ (at % 8))
        source = recouple.at[core, pl.ds(pl.multiple_of(chip_at * seg, seg), seg)]
        copies.append(
            pltpu.make_async_copy(source, rows.at[at * seg : (at + 1) * seg], sems.at[at])
        )
    for copy in copies:
        copy.start()
    for copy in copies:
        copy.wait()


def load_call(sc, recouple, amplitudes, *waits):
    _, n, half = amplitudes.shape
    return pl.pallas_call(
        load_kernel,
        grid_spec=pltpu.PrefetchScalarGridSpec(
            num_scalar_prefetch=1,
            grid=(1,),
            in_specs=[AWAY, AWAY] + [WAIT] * len(waits),
            out_specs=[WHOLE] * 2,
            scratch_shapes=[pltpu.SemaphoreType.DMA((65,))],
        ),
        out_shape=[VMEM((n, n), BF), VMEM((n, half), BF)],
        compiler_params=params(1),
        cost_estimate=cost(0, 4 * n * n),
        name="load",
    )(sc, far(recouple), far(amplitudes), *waits)


def spread(got, i, outs, columns):
    each = 8 // TILES
    seg = outs[0].shape[1]
    for j in range(each):
        piece = got[j * 8 * seg : (j + 1) * 8 * seg]
        outs[i * each + j][:, :, columns] = piece.reshape(8, seg, piece.shape[1])


def own_kernel(rows, amp, *refs):
    outs = refs[-8:]
    tile = rows.shape[0] // TILES
    for i in range(TILES):
        got = dot(rows[i * tile : (i + 1) * tile], amp[...]).astype(BF)
        spread(got, i, outs, slice(0, amp.shape[1]))


def own_call(rows, amp, *waits):
    n, half = amp.shape
    return pl.pallas_call(
        own_kernel,
        in_specs=[WHOLE, WHOLE] + [WAIT] * len(waits),
        out_specs=[WHOLE] * 8,
        out_shape=[VMEM((8, n // 64, 2 * half), BF)] * 8,
        compiler_params=params(4),
        cost_estimate=cost(2 * n * n * half, 2 * n * n),
        name="recoupled_own",
    )(held(rows), held(amp), *waits)


def other_kernel(rows, pair, *refs):
    outs = refs[-8:]
    _, n, half = pair.shape
    tile = n // TILES
    for i in range(TILES):
        got = dot(rows[i * tile : (i + 1) * tile], pair[0]).astype(BF)
        spread(got, i, outs, slice(half, 2 * half))


def other_call(rows, pair, begun, *waits):
    _, n, half = pair.shape
    return pl.pallas_call(
        other_kernel,
        in_specs=[WHOLE] * 10 + [WAIT] * len(waits),
        out_specs=[WHOLE] * 8,
        out_shape=[VMEM(begun[0].shape, BF)] * 8,
        input_output_aliases={2 + r: r for r in range(8)},
        compiler_params=params(4),
        cost_estimate=cost(2 * n * n * half, 4 * n * half),
        name="recoupled_other",
    )(held(rows), held(pair), *[held(block) for block in begun], *waits)


def coupling_kernel(sc, own, oth, *refs):
    out, sems = refs[-2:]
    half = own.shape[1]
    copies = []
    for part, ref in enumerate((own, oth)):
        for side in range(2):
            at = pl.ds(pl.multiple_of((sc[0] ^ side) * half, half), half)
            to = out.at[part * half : (part + 1) * half, side * half : (side + 1) * half]
            copies.append(pltpu.make_async_copy(ref.at[sc[0], :, at], to, sems.at[len(copies)]))
    for copy in copies:
        copy.start()
    for copy in copies:
        copy.wait()


def coupling_call(sc, own, oth, *waits):
    _, half, h = own.shape
    return pl.pallas_call(
        coupling_kernel,
        grid_spec=pltpu.PrefetchScalarGridSpec(
            num_scalar_prefetch=1,
            grid=(1,),
            in_specs=[AWAY, WAIT] + [WAIT] * len(waits),
            out_specs=WHOLE,
            scratch_shapes=[pltpu.SemaphoreType.DMA((4,))],
        ),
        out_shape=VMEM((h, h), BF),
        compiler_params=params(1),
        cost_estimate=cost(0, 4 * h * h),
        name="coupling",
    )(sc, far(own), oth, *waits)


def cycle_kernel(count, *refs):
    blocks, couplings, outs = refs[:count], refs[count : count + 8], refs[-count:]
    seg = blocks[0].shape[1]
    for k in range(8):
        lines = jnp.concatenate([block[k] for block in blocks], axis=0)
        got = dot(lines, couplings[k][...]).astype(BF)
        for r, out in enumerate(outs):
            out[k] = got[r * seg : (r + 1) * seg]


def cycle_call(blocks, couplings, *waits):
    count = len(blocks)
    _, rows, h = blocks[0].shape
    return pl.pallas_call(
        functools.partial(cycle_kernel, count),
        in_specs=[WHOLE] * (count + 8) + [WAIT] * len(waits),
        out_specs=[WHOLE] * count,
        out_shape=[VMEM(blocks[0].shape, BF)] * count,
        compiler_params=params(4),
        cost_estimate=cost(16 * count * rows * h * h, 32 * count * rows * h + 16 * h * h),
        name="cycle",
    )(*[held(b) for b in blocks], *[held(c) for c in couplings], *waits)


def ladder_kernel(tiles, sc, ladder_int, amp, drive, pair, part, *refs):
    out, out_part = refs[-2:]
    core, half, tile = sc[0], amp.shape[1], amp.shape[0] // TILES
    for i in tiles:
        at = slice(i * tile, (i + 1) * tile)
        left = ladder_int[core, at]
        out[at, :half] = dot(left, amp[...]) + drive[core, at].astype(F32)
        out[at, half:] = dot(left, pair[0]) + pair[1, at].astype(F32)
        out_part[at, :] = jnp.broadcast_to(part[pl.ds(core, 1), at], (128, tile)).T


def ladder_call(tiles, begun, operands, *waits):
    n, half = operands[2].shape
    operands = operands[:1] + [held(a) for a in operands[1:]]
    return pl.pallas_call(
        functools.partial(ladder_kernel, tiles),
        grid_spec=pltpu.PrefetchScalarGridSpec(
            num_scalar_prefetch=1,
            grid=(1,),
            in_specs=[WHOLE] * (5 + len(begun)) + [WAIT] * len(waits),
            out_specs=[WHOLE, WHOLE],
        ),
        out_shape=[VMEM((n, 2 * half), F32), VMEM((n, 128), F32)],
        input_output_aliases={6 + i: i for i in range(len(begun))},
        compiler_params=params(4),
        cost_estimate=cost(n * n * half * len(tiles), 8 * n * half),
        name="ladder",
    )(*operands, *[held(array) for array in begun], *waits)


def gathered(blocks, lines, columns):
    rows = blocks[0].shape[0] * blocks[0].shape[1]
    for j, block in enumerate(blocks):
        got = block[:, :, columns]
        lines[j * rows : (j + 1) * rows, :] = got.reshape(rows, got.shape[2])


def folded_kernel(chosen, rows, ladder, *refs):
    blocks, (out, lines) = refs[: len(chosen)], refs[-2:]
    tile = rows.shape[1] // TILES
    gathered(blocks, lines, slice(0, lines.shape[1]))
    for i in range(TILES):
        at = slice(i * tile, (i + 1) * tile)
        out[at] = ladder[at] + folded(chosen, rows, at, lines)


def folded(chosen, rows, at, lines):
    each = rows.shape[0] // 8
    return dot_rows(rows[chosen[0] * each : (chosen[-1] + 1) * each, at], lines[...])


def folded_call(chosen, rows, returned, ladder, *waits):
    n, h = ladder.shape
    part = n * len(chosen) // 8
    return pl.pallas_call(
        functools.partial(folded_kernel, chosen),
        in_specs=[WHOLE] * (2 + len(chosen)) + [WAIT] * len(waits),
        out_specs=WHOLE,
        out_shape=VMEM(ladder.shape, F32),
        input_output_aliases={1: 0},
        scratch_shapes=[VMEM((part, h), BF)],
        compiler_params=params(8),
        cost_estimate=cost(2 * n * part * h, 6 * n * h),
        name="folded",
    )(held(rows), held(ladder), *[held(returned[r]) for r in chosen], *waits)


def final_kernel(chosen, side, sc, rows, ladder, part, hole, *refs):
    blocks, (out, lines, made, sems) = refs[: len(chosen)], refs[-4:]
    n, half = lines.shape[0] * 8 // len(chosen), lines.shape[1]
    tile = n // TILES
    cols = slice(side * half, (side + 1) * half)
    gathered(blocks, lines, cols)
    copies = []
    for i in range(TILES):
        at = slice(i * tile, (i + 1) * tile)
        total = ladder[at, cols] + folded(chosen, rows, at, lines)
        got = (total / (part[at, :1] - hole[pl.ds(sc[0], 1), :])).astype(BF)
        if side == 1:
            out[at] = got
        else:
            made[at] = got
            copies.append(
                pltpu.make_async_copy(made.at[at], out.at[sc[0], at], sems.at[i])
            )
            copies[-1].start()
    for copy in copies:
        copy.wait()


def final_call(chosen, side, sc, rows, returned, ladder, part, hole, *waits):
    n, h = ladder.shape
    half = h // 2
    return pl.pallas_call(
        functools.partial(final_kernel, chosen, side),
        grid_spec=pltpu.PrefetchScalarGridSpec(
            num_scalar_prefetch=1,
            grid=(1,),
            in_specs=[WHOLE] * (4 + len(chosen)) + [WAIT] * len(waits),
            out_specs=WHOLE if side else AWAY,
            scratch_shapes=[
                VMEM((n * len(chosen) // 8, half), BF),
                VMEM((n, half), BF),
                pltpu.SemaphoreType.DMA((TILES,)),
            ],
        ),
        out_shape=VMEM((n, half), BF) if side else pltpu.HBM((2, n, half), BF),
        compiler_params=params(6),
        cost_estimate=cost(2 * n * n * half, 6 * n * half),
        name=("final_own", "final_other")[side],
    )(
        sc,
        held(rows),
        held(ladder),
        held(part),
        held(hole),
        *[held(returned[r]) for r in chosen],
        *waits,
    )


def place_kernel(sc, arrived, given, out, sems):
    each = arrived.shape[0] // TILES
    copies = []
    for i in range(TILES):
        at = slice(i * each, (i + 1) * each)
        copies.append(
            pltpu.make_async_copy(arrived.at[at], out.at[1 - sc[0], at], sems.at[i])
        )
    for copy in copies:
        copy.start()
    for copy in copies:
        copy.wait()


def place_call(sc, arrived, out):
    n, half = arrived.shape
    return pl.pallas_call(
        place_kernel,
        grid_spec=pltpu.PrefetchScalarGridSpec(
            num_scalar_prefetch=1,
            grid=(1,),
            in_specs=[WHOLE, AWAY],
            out_specs=AWAY,
            scratch_shapes=[pltpu.SemaphoreType.DMA((TILES,))],
        ),
        out_shape=pltpu.HBM((2, n, half), BF),
        input_output_aliases={2: 0},
        compiler_params=params(1),
        cost_estimate=cost(0, 4 * n * half),
        name="place",
    )(sc, held(arrived), far(out))


def local(amplitudes, recouple, ladder_int, cycle_coupling, drive, eps_part, eps_hole):
    core, here = lax.axis_index("dom"), lax.axis_index("chan")
    moved = kept = 0
    for first, weight in zip(HIGH, (16, 4, 1)):
        place = (here // weight) % 4
        high, low = place // 2, ((place + 1) // 2) % 2
        moved = 2 * moved + jnp.where(core == 1 - first, high, low)
        kept = 2 * kept + jnp.where(core == 1 - first, low, high)
    sc = jnp.stack([core, kept, moved]).astype(jnp.int32)

    coupling_other = swap(cycle_coupling)
    hole_other = swap(eps_hole)
    pair = cut_call(sc, amplitudes, drive)
    c0 = coupling_call(sc, cycle_coupling, coupling_other, pair, hole_other)
    (pair,) = tie([pair], c0)
    pair = swap(pair)

    c4, c2, c1 = over(c0, kept=4), over(c0, kept=2), over(c0, kept=1)
    rows, amp = load_call(sc, recouple, amplitudes, c0)

    begun = own_call(rows, amp)
    c4, c2, c1 = tie([c4, c2, c1], begun[0])
    c6, c3, c5 = over(c4, kept=2), over(c2, kept=1), over(c1, kept=4)
    send = dict(zip(ORDER, other_call(rows, pair, begun)))

    blocks = {0: send[0]}
    for r in FIRST:
        blocks[r] = over(send[r], moved=r)
    operands = [sc, ladder_int, amp, drive, pair, eps_part]
    ladder = ladder_call((0,), (), operands)

    c6, c3, c5, *rest = tie(
        [c6, c3, c5] + [send[r] for r in THEN], ladder[0], blocks[FIRST[0]]
    )
    c7 = over(c6, kept=1)
    for r, block in zip(THEN, rest):
        blocks[r] = over(block, moved=r)
    ladder, part = ladder_call((1, 2, 3), ladder, operands)

    couplings = [c0, c1, c2, c3, c4, c5, c6, c7]
    returned = []
    for group in BACK:
        cycled = cycle_call([blocks[r] for r in group], couplings, ladder)
        returned += [over(block, moved=r) if r else block for r, block in zip(group, cycled)]
    for group in EARLY:
        ladder = folded_call(group, rows, returned, ladder)
    out_other = final_call(LATE, 1, sc, rows, returned, ladder, part, hole_other)
    out = final_call(LATE, 0, sc, rows, returned, ladder, part, eps_hole, out_other)
    return place_call(sc, swap(out_other), out)


def solution(mesh):
    placed = (
        P("chan", None, "dom"),
        P("chan", None, None),
        P("chan", None, None),
        P("chan", "dom", None),
        P("chan", None, "dom"),
        P("chan", None),
        P("chan", "dom"),
    )
    return jax.shard_map(
        local, mesh=mesh, in_specs=placed, out_specs=P("chan", None, "dom"), check_vma=False
    )
```

```python
import functools
import itertools

import jax
import jax.numpy as jnp
from jax import lax
from jax.experimental import pallas as pl
from jax.experimental.pallas import tpu as pltpu
from jax.sharding import PartitionSpec as P

RING = ((0, 0), (0, 1), (1, 1), (1, 0))
PLACE = {bits: at for at, bits in enumerate(RING)}
BF, F32 = jnp.bfloat16, jnp.float32
VMEM = pltpu.VMEM


def chip(bits):
    return (PLACE[bits[0]] * 4 + PLACE[bits[1]]) * 4 + PLACE[bits[2]]


HIGH = (0, 0, 0)


def bits_of(core, moved, kept):
    return [(m, k) if first ^ core else (k, m) for first, m, k in zip(HIGH, moved, kept)]


THREE = list(itertools.product((0, 1), repeat=3))
def flips(of_moved, of_kept):
    pairs = []
    for core, moved, kept in itertools.product(range(2), THREE, THREE):
        to = [m ^ f for m, f in zip(moved, THREE[of_moved])]
        at = [k ^ f for k, f in zip(kept, THREE[of_kept])]
        pairs.append(
            (
                chip(bits_of(core, moved, kept)) * 2 + core,
                chip(bits_of(core, to, at)) * 2 + core,
            )
        )
    return pairs


BOTH = ("chan", "dom")


def swap(array):
    return lax.ppermute(array, "dom", [(0, 1), (1, 0)])


def over(array, moved=0, kept=0):
    return lax.ppermute(array, BOTH, flips(moved, kept))


def segment(core, moved, kept):
    at = 0
    for first, shift in zip(HIGH, (2, 1, 0)):
        m, k = (moved >> shift) & 1, (kept >> shift) & 1
        at = at * 4 + 2 * jnp.where(core == 1 - first, m, k) + (m ^ k)
    return at


def dot(a, b):
    return jnp.dot(a, b, preferred_element_type=F32)


def dot_rows(a, b):
    return lax.dot_general(a, b, (((0,), (0,)), ((), ())), preferred_element_type=F32)


def params(mib):
    return pltpu.CompilerParams(vmem_limit_bytes=mib * 1024 * 1024)


def cost(flops, moved):
    return pl.CostEstimate(flops=flops, bytes_accessed=moved, transcendentals=0)


def held(array):
    return pltpu.with_memory_space_constraint(array, VMEM)


def far(array):
    return pltpu.with_memory_space_constraint(array, pltpu.HBM)


WHOLE = pl.BlockSpec(memory_space=VMEM)
AWAY = pl.BlockSpec(memory_space=pltpu.HBM)
WAIT = pl.BlockSpec(memory_space=pl.ANY)
TILES = 4
FIRST, THEN = (1, 7), (2, 4, 3, 5, 6)
BACK = (0, 1, 2, 4, 7), (3, 5, 6)
ORDER = BACK[0] + BACK[1]
EARLY, LATE = (range(5), range(5, 6)), range(6, 8)


def tie_kernel(*refs):
    pass


def tie(arrays, *waits):
    count = len(arrays)
    return pl.pallas_call(
        tie_kernel,
        in_specs=[WAIT] * (count + len(waits)),
        out_specs=[WAIT] * count,
        out_shape=[jax.ShapeDtypeStruct(a.shape, a.dtype) for a in arrays],
        input_output_aliases={i: i for i in range(count)},
        compiler_params=params(1),
        cost_estimate=cost(0, 0),
        name="tie",
    )(*arrays, *waits)


def cut_kernel(sc, amplitudes, drive, pair, sems):
    copies = [
        pltpu.make_async_copy(whole.at[1 - sc[0]], pair.at[i], sems.at[i])
        for i, whole in enumerate((amplitudes, drive))
    ]
    for copy in copies:
        copy.start()
    for copy in copies:
        copy.wait()


def cut_call(sc, amplitudes, drive):
    return pl.pallas_call(
        cut_kernel,
        grid_spec=pltpu.PrefetchScalarGridSpec(
            num_scalar_prefetch=1,
            grid=(1,),
            in_specs=[AWAY, AWAY],
            out_specs=WHOLE,
            scratch_shapes=[pltpu.SemaphoreType.DMA((2,))],
        ),
        out_shape=VMEM(amplitudes.shape, BF),
        compiler_params=params(1),
        cost_estimate=cost(0, 8 * amplitudes.shape[1] * amplitudes.shape[2]),
        name="cut",
    )(sc, far(amplitudes), far(drive))


def load_kernel(sc, recouple, amplitudes, *refs):
    rows, amp, sems = refs[-3:]
    core, seg = sc[0], rows.shape[0] // 64
    copies = [pltpu.make_async_copy(amplitudes.at[core], amp, sems.at[64])]
    for at in range(64):
        chip_at = segment(core, sc[2] ^ ORDER[at // 8], sc[1] ^ (at % 8))
        source = recouple.at[core, pl.ds(pl.multiple_of(chip_at * seg, seg), seg)]
        copies.append(
            pltpu.make_async_copy(source, rows.at[at * seg : (at + 1) * seg], sems.at[at])
        )
    for copy in copies:
        copy.start()
    for copy in copies:
        copy.wait()


def load_call(sc, recouple, amplitudes, *waits):
    _, n, half = amplitudes.shape
    return pl.pallas_call(
        load_kernel,
        grid_spec=pltpu.PrefetchScalarGridSpec(
            num_scalar_prefetch=1,
            grid=(1,),
            in_specs=[AWAY, AWAY] + [WAIT] * len(waits),
            out_specs=[WHOLE] * 2,
            scratch_shapes=[pltpu.SemaphoreType.DMA((65,))],
        ),
        out_shape=[VMEM((n, n), BF), VMEM((n, half), BF)],
        compiler_params=params(1),
        cost_estimate=cost(0, 4 * n * n),
        name="load",
    )(sc, far(recouple), far(amplitudes), *waits)


def spread(got, i, outs, columns):
    each = 8 // TILES
    seg = outs[0].shape[1]
    for j in range(each):
        piece = got[j * 8 * seg : (j + 1) * 8 * seg]
        outs[i * each + j][:, :, columns] = piece.reshape(8, seg, piece.shape[1])


def own_kernel(rows, amp, *refs):
    outs = refs[-8:]
    tile = rows.shape[0] // TILES
    for i in range(TILES):
        got = dot(rows[i * tile : (i + 1) * tile], amp[...]).astype(BF)
        spread(got, i, outs, slice(0, amp.shape[1]))


def own_call(rows, amp, *waits):
    n, half = amp.shape
    return pl.pallas_call(
        own_kernel,
        in_specs=[WHOLE, WHOLE] + [WAIT] * len(waits),
        out_specs=[WHOLE] * 8,
        out_shape=[VMEM((8, n // 64, 2 * half), BF)] * 8,
        compiler_params=params(4),
        cost_estimate=cost(2 * n * n * half, 2 * n * n),
        name="recoupled_own",
    )(held(rows), held(amp), *waits)


def other_kernel(rows, pair, *refs):
    outs = refs[-8:]
    _, n, half = pair.shape
    tile = n // TILES
    for i in range(TILES):
        got = dot(rows[i * tile : (i + 1) * tile], pair[0]).astype(BF)
        spread(got, i, outs, slice(half, 2 * half))


def other_call(rows, pair, begun, *waits):
    _, n, half = pair.shape
    return pl.pallas_call(
        other_kernel,
        in_specs=[WHOLE] * 10 + [WAIT] * len(waits),
        out_specs=[WHOLE] * 8,
        out_shape=[VMEM(begun[0].shape, BF)] * 8,
        input_output_aliases={2 + r: r for r in range(8)},
        compiler_params=params(4),
        cost_estimate=cost(2 * n * n * half, 4 * n * half),
        name="recoupled_other",
    )(held(rows), held(pair), *[held(block) for block in begun], *waits)


def coupling_kernel(sc, own, oth, *refs):
    out, sems = refs[-2:]
    half = own.shape[1]
    copies = []
    for part, ref in enumerate((own, oth)):
        for side in range(2):
            at = pl.ds(pl.multiple_of((sc[0] ^ side) * half, half), half)
            to = out.at[part * half : (part + 1) * half, side * half : (side + 1) * half]
            copies.append(pltpu.make_async_copy(ref.at[sc[0], :, at], to, sems.at[len(copies)]))
    for copy in copies:
        copy.start()
    for copy in copies:
        copy.wait()


def coupling_call(sc, own, oth, *waits):
    _, half, h = own.shape
    return pl.pallas_call(
        coupling_kernel,
        grid_spec=pltpu.PrefetchScalarGridSpec(
            num_scalar_prefetch=1,
            grid=(1,),
            in_specs=[AWAY, WAIT] + [WAIT] * len(waits),
            out_specs=WHOLE,
            scratch_shapes=[pltpu.SemaphoreType.DMA((4,))],
        ),
        out_shape=VMEM((h, h), BF),
        compiler_params=params(1),
        cost_estimate=cost(0, 4 * h * h),
        name="coupling",
    )(sc, far(own), oth, *waits)


def cycle_kernel(count, *refs):
    blocks, couplings, outs = refs[:count], refs[count : count + 8], refs[-count:]
    seg = blocks[0].shape[1]
    for k in range(8):
        lines = jnp.concatenate([block[k] for block in blocks], axis=0)
        got = dot(lines, couplings[k][...]).astype(BF)
        for r, out in enumerate(outs):
            out[k] = got[r * seg : (r + 1) * seg]


def cycle_call(blocks, couplings, *waits):
    count = len(blocks)
    _, rows, h = blocks[0].shape
    return pl.pallas_call(
        functools.partial(cycle_kernel, count),
        in_specs=[WHOLE] * (count + 8) + [WAIT] * len(waits),
        out_specs=[WHOLE] * count,
        out_shape=[VMEM(blocks[0].shape, BF)] * count,
        compiler_params=params(4),
        cost_estimate=cost(16 * count * rows * h * h, 32 * count * rows * h + 16 * h * h),
        name="cycle",
    )(*[held(b) for b in blocks], *[held(c) for c in couplings], *waits)


def ladder_kernel(tiles, sc, ladder_int, amp, drive, pair, part, *refs):
    out, out_part = refs[-2:]
    core, half, tile = sc[0], amp.shape[1], amp.shape[0] // TILES
    for i in tiles:
        at = slice(i * tile, (i + 1) * tile)
        left = ladder_int[core, at]
        out[at, :half] = dot(left, amp[...]) + drive[core, at].astype(F32)
        out[at, half:] = dot(left, pair[0]) + pair[1, at].astype(F32)
        out_part[at, :] = jnp.broadcast_to(part[pl.ds(core, 1), at], (128, tile)).T


def ladder_call(tiles, begun, operands, *waits):
    n, half = operands[2].shape
    operands = operands[:1] + [held(a) for a in operands[1:]]
    return pl.pallas_call(
        functools.partial(ladder_kernel, tiles),
        grid_spec=pltpu.PrefetchScalarGridSpec(
            num_scalar_prefetch=1,
            grid=(1,),
            in_specs=[WHOLE] * (5 + len(begun)) + [WAIT] * len(waits),
            out_specs=[WHOLE, WHOLE],
        ),
        out_shape=[VMEM((n, 2 * half), F32), VMEM((n, 128), F32)],
        input_output_aliases={6 + i: i for i in range(len(begun))},
        compiler_params=params(4),
        cost_estimate=cost(n * n * half * len(tiles), 8 * n * half),
        name="ladder",
    )(*operands, *[held(array) for array in begun], *waits)


def gathered(blocks, lines, columns):
    rows = blocks[0].shape[0] * blocks[0].shape[1]
    for j, block in enumerate(blocks):
        got = block[:, :, columns]
        lines[j * rows : (j + 1) * rows, :] = got.reshape(rows, got.shape[2])


def folded_kernel(chosen, rows, ladder, *refs):
    blocks, (out, lines) = refs[: len(chosen)], refs[-2:]
    tile = rows.shape[1] // TILES
    gathered(blocks, lines, slice(0, lines.shape[1]))
    for i in range(TILES):
        at = slice(i * tile, (i + 1) * tile)
        out[at] = ladder[at] + folded(chosen, rows, at, lines)


def folded(chosen, rows, at, lines):
    each = rows.shape[0] // 8
    return dot_rows(rows[chosen[0] * each : (chosen[-1] + 1) * each, at], lines[...])


def folded_call(chosen, rows, returned, ladder, *waits):
    n, h = ladder.shape
    part = n * len(chosen) // 8
    return pl.pallas_call(
        functools.partial(folded_kernel, chosen),
        in_specs=[WHOLE] * (2 + len(chosen)) + [WAIT] * len(waits),
        out_specs=WHOLE,
        out_shape=VMEM(ladder.shape, F32),
        input_output_aliases={1: 0},
        scratch_shapes=[VMEM((part, h), BF)],
        compiler_params=params(8),
        cost_estimate=cost(2 * n * part * h, 6 * n * h),
        name="folded",
    )(held(rows), held(ladder), *[held(returned[r]) for r in chosen], *waits)


def final_kernel(chosen, side, sc, rows, ladder, part, hole, *refs):
    blocks, (out, lines, made, sems) = refs[: len(chosen)], refs[-4:]
    n, half = lines.shape[0] * 8 // len(chosen), lines.shape[1]
    tile = n // TILES
    cols = slice(side * half, (side + 1) * half)
    gathered(blocks, lines, cols)
    copies = []
    for i in range(TILES):
        at = slice(i * tile, (i + 1) * tile)
        total = ladder[at, cols] + folded(chosen, rows, at, lines)
        got = (total / (part[at, :1] - hole[pl.ds(sc[0], 1), :])).astype(BF)
        if side == 1:
            out[at] = got
        else:
            made[at] = got
            copies.append(
                pltpu.make_async_copy(made.at[at], out.at[sc[0], at], sems.at[i])
            )
            copies[-1].start()
    for copy in copies:
        copy.wait()


def final_call(chosen, side, sc, rows, returned, ladder, part, hole, *waits):
    n, h = ladder.shape
    half = h // 2
    return pl.pallas_call(
        functools.partial(final_kernel, chosen, side),
        grid_spec=pltpu.PrefetchScalarGridSpec(
            num_scalar_prefetch=1,
            grid=(1,),
            in_specs=[WHOLE] * (4 + len(chosen)) + [WAIT] * len(waits),
            out_specs=WHOLE if side else AWAY,
            scratch_shapes=[
                VMEM((n * len(chosen) // 8, half), BF),
                VMEM((n, half), BF),
                pltpu.SemaphoreType.DMA((TILES,)),
            ],
        ),
        out_shape=VMEM((n, half), BF) if side else pltpu.HBM((2, n, half), BF),
        compiler_params=params(6),
        cost_estimate=cost(2 * n * n * half, 6 * n * half),
        name=("final_own", "final_other")[side],
    )(
        sc,
        held(rows),
        held(ladder),
        held(part),
        held(hole),
        *[held(returned[r]) for r in chosen],
        *waits,
    )


def place_kernel(sc, arrived, given, out, sems):
    each = arrived.shape[0] // TILES
    copies = []
    for i in range(TILES):
        at = slice(i * each, (i + 1) * each)
        copies.append(
            pltpu.make_async_copy(arrived.at[at], out.at[1 - sc[0], at], sems.at[i])
        )
    for copy in copies:
        copy.start()
    for copy in copies:
        copy.wait()


def place_call(sc, arrived, out):
    n, half = arrived.shape
    return pl.pallas_call(
        place_kernel,
        grid_spec=pltpu.PrefetchScalarGridSpec(
            num_scalar_prefetch=1,
            grid=(1,),
            in_specs=[WHOLE, AWAY],
            out_specs=AWAY,
            scratch_shapes=[pltpu.SemaphoreType.DMA((TILES,))],
        ),
        out_shape=pltpu.HBM((2, n, half), BF),
        input_output_aliases={2: 0},
        compiler_params=params(1),
        cost_estimate=cost(0, 4 * n * half),
        name="place",
    )(sc, held(arrived), far(out))


def local(amplitudes, recouple, ladder_int, cycle_coupling, drive, eps_part, eps_hole):
    core, here = lax.axis_index("dom"), lax.axis_index("chan")
    moved = kept = 0
    for first, weight in zip(HIGH, (16, 4, 1)):
        place = (here // weight) % 4
        high, low = place // 2, ((place + 1) // 2) % 2
        moved = 2 * moved + jnp.where(core == 1 - first, high, low)
        kept = 2 * kept + jnp.where(core == 1 - first, low, high)
    sc = jnp.stack([core, kept, moved]).astype(jnp.int32)

    coupling_other = swap(cycle_coupling)
    hole_other = swap(eps_hole)
    pair = cut_call(sc, amplitudes, drive)
    c0 = coupling_call(sc, cycle_coupling, coupling_other, pair, hole_other)
    (pair,) = tie([pair], c0)
    pair = swap(pair)

    c4, c2, c1 = over(c0, kept=4), over(c0, kept=2), over(c0, kept=1)
    rows, amp = load_call(sc, recouple, amplitudes, c0)

    begun = own_call(rows, amp)
    c4, c2, c1 = tie([c4, c2, c1], begun[0])
    c6, c3, c5 = over(c4, kept=2), over(c2, kept=1), over(c1, kept=4)
    send = dict(zip(ORDER, other_call(rows, pair, begun)))

    blocks = {0: send[0]}
    for r in FIRST:
        blocks[r] = over(send[r], moved=r)
    operands = [sc, ladder_int, amp, drive, pair, eps_part]
    ladder = ladder_call((0,), (), operands)

    c6, c3, c5, *rest = tie(
        [c6, c3, c5] + [send[r] for r in THEN], ladder[0], blocks[FIRST[0]]
    )
    c7 = over(c6, kept=1)
    for r, block in zip(THEN, rest):
        blocks[r] = over(block, moved=r)
    ladder, part = ladder_call((1, 2, 3), ladder, operands)

    couplings = [c0, c1, c2, c3, c4, c5, c6, c7]
    returned = []
    for group in BACK:
        cycled = cycle_call([blocks[r] for r in group], couplings, ladder)
        returned += [over(block, moved=r) if r else block for r, block in zip(group, cycled)]
    for group in EARLY:
        ladder = folded_call(group, rows, returned, ladder)
    out_other = final_call(LATE, 1, sc, rows, returned, ladder, part, hole_other)
    out = final_call(LATE, 0, sc, rows, returned, ladder, part, eps_hole, out_other)
    return place_call(sc, swap(out_other), out)


def solution(mesh):
    placed = (
        P("chan", None, "dom"),
        P("chan", None, None),
        P("chan", None, None),
        P("chan", "dom", None),
        P("chan", None, "dom"),
        P("chan", None),
        P("chan", "dom"),
    )
    return jax.shard_map(
        local, mesh=mesh, in_specs=placed, out_specs=P("chan", None, "dom"), check_vma=False
    )
```
